256 devices in a mesh: dp: 32 (over z, y_lo, core), tensor: 8 (over x, y_hi).
Axes of the slice: x: 4, y: 4 (y_hi: 2, y_lo: 2; y = y_hi * 2 + y_lo), z: 8, core: 2. Of those that a mesh axis runs over, the one named last changes fastest.
Arguments:
- hidden: bfloat16 [32768, 14336], P('dp', 'tensor'), may hold values from -6 to 6
- cotangent: bfloat16 [32768, 4096], P('dp', 'tensor'), may hold values from -0.03125 to 0.03125
- weight_slots: bfloat16 [8, 32, 10, 128, 128], P('tensor', 'dp'), may hold values from -0.0625 to 0.0625
- pattern: int32 [112, 16], P('tensor'), may hold values from 0 to 31, all different within a row
- owners: int32 [112, 16, 1], P('tensor'), may hold values from 0 to 31; in each aligned block of 224 rows (0 to 223, 224 to 447, ..., all dimensions but the last counted through in order) at most 10 rows name the same one
- first_moment: float32 [8, 32, 10, 128, 128], P('tensor', 'dp'), may hold values from -3 to 3
- second_moment: float32 [8, 32, 10, 128, 128], P('tensor', 'dp'), may hold values from 0.05 to 2
- next_hidden: bfloat16 [4096, 14336], P('dp', 'tensor'), may hold values from -6 to 6
Outputs:
- next_out: bfloat16 [4096, 4096], P('dp', 'tensor')
- new_first: float32 [8, 32, 10, 128, 128], P('tensor', 'dp')
- new_second: float32 [8, 32, 10, 128, 128], P('tensor', 'dp')
The draws below stay inside these ranges and needn't reach their ends.
Inputs may be any that keep to these rules, and one draw needn't show every extreme that they name: `pattern`: each row names 16 different column blocks. `owners`: among the 224 blocks of one tensor index no dp index owns more than 10, and in some tensor index one dp index owns exactly 10.
All inputs are finite; a program needn't handle non-finite values.
Results may differ from the reference program's by a relative error of at most 0.018.
Values may be sent and summed in bfloat16 or wider, within the bound.
A program may use at most 192 MiB of HBM per device.

```python
import math
import jax
import jax.numpy as jnp
import numpy as np
from jax import lax

D = 4096
FF = 14336
BLK = 128
ADAM_STEP = 20
TOK_DEV = 1024
DB = 32
KEEP = 16
FB = 112
LOCAL_BLOCKS = 224
OWN_MAX = 10
TOKENS = 32768
NEXT_TOKENS = 4096
N_DP = 32
N_TENSOR = 8


def level_of(stream_key, shape, cuts, least, largest):
    gain = 1.0
    for dim, shards_of in cuts:
        steps = jax.random.uniform(jax.random.fold_in(jax.random.fold_in(stream_key, 6), dim), (shards_of,), jnp.float32, least / len(cuts), largest / len(cuts))
        gain = gain * jnp.repeat(jnp.exp(steps), shape[dim] // shards_of).reshape((-1,) + (1,) * (len(shape) - 1 - dim))
    return gain


def picks_of(own_key, rows, amount, top, lift):
    order = jax.random.permutation(jax.random.fold_in(own_key, 1), amount)
    pull = order
    for power in range(3):
        pull = pull * pull // amount
    pull = pull * lift // amount
    chance = jax.random.randint(jax.random.fold_in(own_key, 2), (rows, amount), 0, 4096) + pull
    fixed_rows = jax.random.permutation(jax.random.fold_in(own_key, 3), rows)[jnp.arange(amount) % rows]
    chance = jnp.where(jnp.arange(rows)[:, None] == fixed_rows[None, :], 1 << 14, chance)
    score = chance * amount + jnp.arange(amount)
    return lax.top_k(score.astype(jnp.int32), top)[1].astype(jnp.int32)


def shared_out(rng, own, number, rows, amount, top, limit, lean):
    ranking = jax.random.permutation(rng, amount)
    heavy_load, usual = shares(amount, rows * top, limit, lean, True), shares(amount, rows * top, limit, lean, False)
    places = jnp.arange(amount)

    def named(sizes, turn):
        used = int((sizes > 0).sum())
        fixed = max(1, used // 4)
        passed = fixed + (places - fixed + turn * (used - fixed)) % max(1, amount - fixed)
        return jnp.zeros((amount,), jnp.int32).at[ranking[jnp.where(places < fixed, places, passed)]].set(jnp.asarray(sizes, jnp.int32))

    sizes = jnp.where(number % 4 == 0, named(heavy_load, number // 4), named(usual, number - number // 4 - 1))
    mixed = jax.random.permutation(jax.random.fold_in(own, 3), amount)
    giver, taker = mixed[0:amount // 2 * 2:2], mixed[1:amount // 2 * 2:2]
    room = jnp.minimum(sizes[giver] - 1, limit - sizes[taker]) // 2
    room = jnp.where((giver == ranking[0]) | (taker == ranking[0]) | (sizes[taker] == 0), 0, jnp.maximum(room, 0))
    passed = jax.random.randint(jax.random.fold_in(own, 4), (amount // 2,), 0, 1 << 20) % (room + 1)
    sizes = sizes.at[giver].add(-passed).at[taker].add(passed)
    members = jnp.searchsorted(jnp.cumsum(sizes), jnp.arange(rows * top), side="right").astype(jnp.int32)
    grid = members.reshape(top, rows).T
    grid = grid[jax.random.permutation(jax.random.fold_in(own, 1), rows)]
    turn = jax.random.randint(jax.random.fold_in(own, 2), (rows, 1), 0, top)
    return jnp.take_along_axis(grid, (jnp.arange(top)[None, :] + turn) % top, axis=1)


def shares(number_of, total, most, skew, full):
    portions = [(1 << 20) // math.isqrt(grade ** skew) + 1 for grade in range(1, number_of + 1)]
    largest = most if full else min(most, max(-(-total // number_of), total * portions[0] // sum(portions)))
    least = 1 if total - largest >= number_of - 1 else 0
    given, surplus = [largest] + [least] * (number_of - 1), total - largest - least * (number_of - 1)
    while surplus > 0:
        candidates = [i for i in range(1, number_of) if given[i] < largest] or [i for i in range(1, number_of) if given[i] < most]
        mass, remaining = sum([portions[i] for i in candidates]), surplus
        for i in candidates:
            addition = min(most - given[i], max(1, remaining * portions[i] // mass), surplus)
            given[i] = given[i] + addition
            surplus = surplus - addition
    return np.array(given)


def centred(own_key, dims, deviation, bound, cuts=(), kind=jnp.bfloat16):
    gain = level_of(own_key, dims, cuts, -0.22, 0.18) if cuts else 1.0
    drawn = jax.random.normal(own_key, dims, jnp.float32) * deviation * gain
    return jnp.minimum(jnp.maximum(drawn, -bound), bound).astype(kind)


def setup_inputs(seed: int = 0) -> dict:
    key_list = jax.random.split(jax.random.key(seed), 9)
    hidden = centred(key_list[0], (TOKENS, FF), 1.0, 6.0, ((0, 32), (1, 8)))
    cotangent = centred(key_list[1], (TOKENS, D), ((TOK_DEV * N_DP) ** -0.5), 0.03125, ((0, 32), (1, 8)))
    weight_slots = centred(key_list[2], (N_TENSOR, N_DP, OWN_MAX, BLK, BLK), (FF // 2) ** -0.5, 0.0625, ((0, 8), (1, 32)))
    pattern = picks_of(key_list[3], FB, DB, KEEP, 0)
    owners_keys = jax.random.split(jax.random.fold_in(key_list[4], 1), FB * KEEP // LOCAL_BLOCKS)
    owners_turns = jax.random.permutation(jax.random.fold_in(key_list[4], 3), FB * KEEP // LOCAL_BLOCKS)
    owners = jax.vmap(lambda own, number: shared_out(jax.random.fold_in(key_list[4], 2), own, number, LOCAL_BLOCKS, N_DP, 1, OWN_MAX, 1))(owners_keys, owners_turns).reshape((FB, KEEP, 1))
    first_moment = centred(key_list[5], (N_TENSOR, N_DP, OWN_MAX, BLK, BLK), 0.5, 3.0, ((0, 8), (1, 32)), jnp.float32)
    second_moment = jnp.clip(jnp.exp(math.log(2.0) - 3.6888794 * jax.random.uniform(key_list[6], (N_TENSOR, N_DP, OWN_MAX, BLK, BLK), jnp.float32) ** level_of(key_list[6], (N_TENSOR, N_DP, OWN_MAX, BLK, BLK), ((0, 8), (1, 32)), -0.2, 0.2)), 0.05, 2.0)
    next_hidden = centred(key_list[7], (NEXT_TOKENS, FF), 1.0, 6.0, ((0, 32), (1, 8)))
    return {"hidden": hidden, "cotangent": cotangent, "weight_slots": weight_slots, "pattern": pattern, "owners": owners, "first_moment": first_moment, "second_moment": second_moment, "next_hidden": next_hidden}


beta_one = 0.9
beta_two = 0.95
learn_rate = 0.003
epsilon = 1e-08

def slot_places(owners):
    per_tensor = owners.reshape(N_TENSOR, -1)
    member = (per_tensor[:, :, None] == jnp.arange(N_DP, dtype=jnp.int32)[None, None, :]).astype(jnp.int32)
    before = jnp.cumsum(member, axis=1) - member
    position = lax.optimization_barrier(jnp.sum(before * member, axis=2))
    return position.reshape(-1).astype(jnp.int32)

def reference(hidden, cotangent, weight_slots, pattern, owners, first_moment, second_moment, next_hidden):
    block_size = weight_slots.shape[3]
    row_blocks, keep_count = pattern.shape
    column_blocks = cotangent.shape[1] // block_size
    hidden_dev = hidden.reshape(N_DP, TOK_DEV, row_blocks, block_size)
    cot_dev = cotangent.reshape(N_DP, TOK_DEV, column_blocks, block_size)

    def accumulate(total, pieces):
        hidden_part, cot_part = pieces
        selected = cot_part[:, pattern].astype(jnp.float32)
        partial_value = jnp.einsum('tfi,tfkj->fkij', hidden_part.astype(jnp.float32), selected)
        rounded = lax.optimization_barrier(partial_value.astype(jnp.bfloat16))
        return (total + rounded.astype(jnp.float32), None)
    start_total = jnp.zeros((row_blocks, keep_count, block_size, block_size), jnp.float32)
    gradient, _ = lax.scan(accumulate, start_total, (hidden_dev, cot_dev))
    gradient = gradient.reshape(row_blocks * keep_count, block_size, block_size)
    owner_flat = owners.reshape(-1).astype(jnp.int32)
    tensor_flat = (jnp.arange(row_blocks * keep_count, dtype=jnp.int32) // LOCAL_BLOCKS).astype(jnp.int32)
    position = slot_places(owners)
    moment_one = first_moment[tensor_flat, owner_flat, position]
    moment_two = second_moment[tensor_flat, owner_flat, position]
    fresh_one = beta_one * moment_one + (1 - beta_one) * gradient
    fresh_two = beta_two * moment_two + (1 - beta_two) * gradient * gradient
    scale_one = 1.0 - beta_one ** ADAM_STEP
    scale_two = 1.0 - beta_two ** ADAM_STEP
    old_weights = weight_slots[tensor_flat, owner_flat, position].astype(jnp.float32)
    stepped = old_weights - learn_rate * (fresh_one / scale_one) / (jnp.sqrt(fresh_two / scale_two) + epsilon)
    new_blocks = stepped.astype(jnp.bfloat16).reshape(row_blocks, keep_count, block_size, block_size)
    new_first = jnp.zeros_like(first_moment).at[tensor_flat, owner_flat, position].set(fresh_one)
    new_second = jnp.zeros_like(second_moment).at[tensor_flat, owner_flat, position].set(fresh_two)
    row_index = jnp.broadcast_to(jnp.arange(row_blocks, dtype=jnp.int32)[:, None], pattern.shape)
    dense = jnp.zeros((row_blocks, column_blocks, block_size, block_size), jnp.bfloat16)
    dense = dense.at[row_index, pattern].set(new_blocks)
    dense = dense.transpose(0, 2, 1, 3).reshape(row_blocks * block_size, column_blocks * block_size)
    next_out = jnp.dot(next_hidden, dense, preferred_element_type=jnp.float32).astype(jnp.bfloat16)
    return (next_out, new_first, new_second)
```

```python
import functools

import jax
import jax.numpy as jnp
from jax import lax
from jax.experimental import pallas as pl
from jax.experimental.pallas import tpu as pltpu
from jax.sharding import PartitionSpec as P

ADAM_STEP = 20
BETA_ONE = 0.9
BETA_TWO = 0.95
LEARN_RATE = 0.003
EPSILON = 1e-08

BLK = 128
CHUNKS = 4
MESH = pl.DeviceIdType.MESH
f32 = jnp.float32
bf16 = jnp.bfloat16


def remote(src, dst, send, recv, where):
    return pltpu.make_async_remote_copy(
        src_ref=src, dst_ref=dst, send_sem=send, recv_sem=recv, device_id=where, device_id_type=MESH
    )


def greet(places):
    barrier = pltpu.get_barrier_semaphore()
    for where in places:
        pl.semaphore_signal(barrier, inc=1, device_id=where, device_id_type=MESH)
    pl.semaphore_wait(barrier, len(places))


class Place:
    def __init__(self, nz, nx):
        self.nz, self.nx = nz, nx
        self.d = lax.axis_index("dp")
        self.t = lax.axis_index("tensor")
        self.z = lax.div(self.d, 4)
        self.yl = lax.rem(lax.div(self.d, 2), 2)
        self.core = lax.rem(self.d, 2)
        self.x = lax.div(self.t, 2)
        self.yh = lax.rem(self.t, 2)

    def dp_of(self, z, yl, core):
        return (z * 2 + yl) * 2 + core

    def tensor_of(self, x, yh):
        return x * 2 + yh

    def x_step(self, k):
        return lax.rem(self.x + (k + self.nx), self.nx)

    def z_step(self, k):
        return lax.rem(self.z + (k + self.nz), self.nz)


def grad_kernel(
    nz, nx, slots, row_blocks,
    tab, cnt, hid, cot, wgt, m1, m2,
    new1, new2, panels,
    cotbuf, hid_t, dense, sendb, recvb, ringb, yrecv,
    ys, yr, xs, xr, fs, fr, ds, dr, rs, rr, ls, lr,
):
    me = Place(nz, nx)
    tokens = cot.shape[0]
    rows = tokens // CHUNKS
    half = rows // 2
    n_dense = dense.shape[0] - 1
    hs = slots // 2

    y_far = {"tensor": me.tensor_of(me.x, 1 - me.yh)}
    x_next = [{"tensor": me.tensor_of(me.x_step(1), me.yh)}, {"tensor": me.tensor_of(me.x_step(-1), me.yh)}]
    z_next = [{"dp": me.dp_of(me.z_step(1), me.yl, me.core)}, {"dp": me.dp_of(me.z_step(-1), me.yl, me.core)}]
    y_near = {"dp": me.dp_of(me.z, 1 - me.yl, me.core)}
    twin = {"dp": me.dp_of(me.z, me.yl, 1 - me.core)}
    greet([y_far] + x_next + z_next + [y_near, twin])

    t_item = [me.t, me.tensor_of(me.x, 1 - me.yh)]

    def t_from(item, q):
        yh = me.yh if item == 0 else 1 - me.yh
        return me.tensor_of(me.x_step(-1 if q == 0 else 1), yh)

    def ycopy(c):
        r = pl.ds(c * rows, rows)
        return remote(cot.at[r], cotbuf.at[me.t, r], ys.at[c], yr.at[c], y_far)

    def xcopy(item, q, c):
        r = pl.ds(c * rows, rows)
        src = cot.at[r] if item == 0 else cotbuf.at[t_item[1], r]
        return remote(src, cotbuf.at[t_item[item], r], xs.at[item, q, c], xr.at[item, q, c], x_next[q])

    def fcopy(item, q, c):
        r = pl.ds(c * rows + q * half, half)
        there = cotbuf.at[t_from(item, q), r]
        return remote(there, there, fs.at[item, q, c], fr.at[item, q, c], x_next[q])

    def group(src, tq):
        def body(i, carry):
            out = jnp.dot(hid_t[pl.ds(i * 256, 256), :], src[...], preferred_element_type=f32)
            for b in range(4):
                for a in range(2):
                    dense[(tq * 4 + b) * row_blocks + 2 * i + a] = out[
                        a * BLK : (a + 1) * BLK, b * BLK : (b + 1) * BLK
                    ].astype(bf16)
            return carry

        lax.fori_loop(0, row_blocks // 2, body, 0)

    for c in range(CHUNKS):
        ycopy(c).start()
        for q in range(2):
            xcopy(0, q, c).start()

    for f in range(row_blocks):
        hid_t[f * BLK : (f + 1) * BLK, :] = hid[:, f * BLK : (f + 1) * BLK].T
    dense[n_dense] = jnp.zeros((BLK, BLK), bf16)
    group(cot, me.t)

    for c in range(CHUNKS):
        for q in range(2):
            xcopy(0, q, c).wait_recv()
            fcopy(0, q, c).start()
        ycopy(c).wait_recv()
        for q in range(2):
            xcopy(1, q, c).start()
    group(cotbuf.at[t_from(0, 0)], t_from(0, 0))
    for q in range(2):
        xcopy(1, q, 0).wait_recv()
        fcopy(1, q, 0).start()
    group(cotbuf.at[t_from(0, 1)], t_from(0, 1))
    for q in range(2):
        xcopy(1, q, 1).wait_recv()
        fcopy(1, q, 1).start()
    group(cotbuf.at[t_item[1]], t_item[1])
    for c in range(2, CHUNKS):
        for q in range(2):
            xcopy(1, q, c).wait_recv()
            fcopy(1, q, c).start()
    x_opp = me.x_step(2)
    t_opp = [me.tensor_of(x_opp, me.yh), me.tensor_of(x_opp, 1 - me.yh)]
    for q in range(2):
        for c in range(CHUNKS):
            fcopy(0, q, c).wait_recv()
    group(cotbuf.at[t_opp[0]], t_opp[0])
    for q in range(2):
        group(cotbuf.at[t_from(1, q)], t_from(1, q))
    for q in range(2):
        for c in range(CHUNKS):
            fcopy(1, q, c).wait_recv()
    group(cotbuf.at[t_opp[1]], t_opp[1])

    def dest_z(s, q):
        return lax.rem(me.z + (2 * nz - 1 - s), nz) if q == 0 else lax.rem(me.z + 1 + s, nz)

    def base_of(s, q, u, core):
        yl = 1 - me.yl if u == 0 else me.yl
        return me.dp_of(dest_z(s, q), yl, core) * slots + q * hs

    def dcopy(s, q):
        return remote(sendb.at[s, q], recvb.at[s, q], ds.at[s, q], dr.at[s, q], twin)

    def rcopy(s, q, u):
        return remote(recvb.at[s, q, u], ringb.at[s, q, u], rs.at[s, q, u], rr.at[s, q, u], z_next[q])

    def lcopy(q):
        return remote(recvb.at[nz - 1, q, 0], yrecv.at[q], ls.at[q], lr.at[q], y_near)

    def fill(s, carry):
        for q in range(2):
            for u in range(2):
                base = base_of(s, q, u, 1 - me.core)
                for i in range(hs):
                    sendb[s, q, u, i] = dense[tab[base + i]]
            dcopy(s, q).start()
        return carry

    lax.fori_loop(0, nz, fill, 0)

    def add(s, q, u, first):
        base = base_of(s, q, u, me.core)
        for i in range(hs):
            v = recvb[s, q, u, i].astype(f32) + dense[tab[base + i]].astype(f32)
            if not first:
                v = v + ringb[s - 1, q, u, i].astype(f32)
            recvb[s, q, u, i] = v.astype(bf16)

    for q in range(2):
        dcopy(0, q).wait_recv()
        for u in range(2):
            add(0, q, u, True)
            rcopy(0, q, u).start()

    def ring(s, carry):
        for q in range(2):
            dcopy(s, q).wait_recv()
        for u in range(2):
            for q in range(2):
                rcopy(s - 1, q, u).wait_recv()
                add(s, q, u, False)
                rcopy(s, q, u).start()
        return carry

    lax.fori_loop(1, nz - 1, ring, 0)
    for q in range(2):
        dcopy(nz - 1, q).wait_recv()
    for u in range(2):
        for q in range(2):
            rcopy(nz - 2, q, u).wait_recv()
            add(nz - 1, q, u, False)
            if u == 0:
                lcopy(q).start()

    scale_one = 1.0 - BETA_ONE**ADAM_STEP
    scale_two = 1.0 - BETA_TWO**ADAM_STEP
    mine = cnt[me.d]
    for q in range(2):
        lcopy(q).wait_recv()
        for i in range(hs):
            k = q * hs + i
            grad = recvb[nz - 1, q, 1, i].astype(f32) + yrecv[q, i].astype(f32)
            used = k < mine
            one = jnp.where(used, BETA_ONE * m1[k] + (1 - BETA_ONE) * grad, 0.0)
            two = jnp.where(used, BETA_TWO * m2[k] + (1 - BETA_TWO) * grad * grad, 0.0)
            new1[k] = one
            new2[k] = two
            step = LEARN_RATE * (one / scale_one) / (jnp.sqrt(two / scale_two) + EPSILON)
            panels[k] = (wgt[k].astype(f32) - step).astype(bf16)

    for c in range(CHUNKS):
        ycopy(c).wait_send()
        for q in range(2):
            for item in range(2):
                xcopy(item, q, c).wait_send()
                fcopy(item, q, c).wait_send()
    for q in range(2):
        lcopy(q).wait_send()

    def drain(s, carry):
        for q in range(2):
            dcopy(s, q).wait_send()
        return carry

    def drain_ring(s, carry):
        for q in range(2):
            for u in range(2):
                rcopy(s, q, u).wait_send()
        return carry

    lax.fori_loop(0, nz, drain, 0)
    lax.fori_loop(0, nz - 1, drain_ring, 0)


def next_kernel(
    nz, nx, slots, row_blocks,
    tab, panel, nxt,
    out,
    pan, wide, outb, rcv,
    ys, yr, rs, rr, ds, dr, ts, tr,
):
    me = Place(nz, nx)
    nt = 2 * nx
    hs = slots // 2
    n_pan = nz * 4 * slots

    z_next = [{"dp": me.dp_of(me.z_step(1), me.yl, me.core)}, {"dp": me.dp_of(me.z_step(-1), me.yl, me.core)}]
    y_near = {"dp": me.dp_of(me.z, 1 - me.yl, me.core)}
    twin = {"dp": me.dp_of(me.z, me.yl, 1 - me.core)}
    peers = [{"tensor": lax.rem(me.t + 1 + m, nt)} for m in range(nt - 1)]
    greet(z_next + [y_near, twin] + peers)

    def place(s, q, u):
        z = lax.rem(me.z + (2 * nz - s), nz) if q == 0 else lax.rem(me.z + s, nz)
        yl = me.yl if u == 0 else 1 - me.yl
        return pan.at[pl.ds(me.dp_of(z, yl, me.core) * slots + q * hs, hs)]

    def ycopy(q):
        return remote(panel.at[pl.ds(q * hs, hs)], place(0, q, 0), ys.at[q], yr.at[q], y_near)

    def rcopy(s, q, u):
        here = place(s, q, u)
        src = panel.at[pl.ds(q * hs, hs)] if (isinstance(s, int) and s == 0 and u == 0) else here
        return remote(src, here, rs.at[s, q, u], rr.at[s, q, u], z_next[q])

    def dcopy(s, q, u):
        here = place(s, q, u)
        src = panel.at[pl.ds(q * hs, hs)] if (isinstance(s, int) and s == 0 and u == 0) else here
        return remote(src, here, ds.at[s, q, u], dr.at[s, q, u], twin)

    for q in range(2):
        ycopy(q).start()
        rcopy(0, q, 0).start()
    for q in range(2):
        dcopy(0, q, 0).start()
    for i in range(slots):
        pan[me.d * slots + i] = panel[i]
    pan[n_pan] = jnp.zeros((BLK, BLK), bf16)
    for q in range(2):
        ycopy(q).wait_recv()
        rcopy(0, q, 1).start()
        dcopy(0, q, 1).start()

    def hop(s, carry):
        for u in range(2):
            for q in range(2):
                rcopy(s - 1, q, u).wait_recv()
                rcopy(s, q, u).start()
                dcopy(s, q, u).start()
        return carry

    lax.fori_loop(1, nz - 1, hop, 0)
    for u in range(2):
        for q in range(2):
            rcopy(nz - 2, q, u).wait_recv()
            dcopy(nz - 1, q, u).start()

    def landed(s, carry):
        for u in range(2):
            for q in range(2):
                dcopy(s, q, u).wait_recv()
        return carry

    lax.fori_loop(0, nz, landed, 0)

    def tcopy(m):
        return remote(outb.at[m], rcv.at[m], ts.at[m], tr.at[m], peers[m])

    total = None
    for m in range(nt):
        tq = lax.rem(me.t + 1 + m, nt)
        buf = m % 2

        def build(f, carry):
            for b in range(4):
                wide[buf, pl.ds(f * BLK, BLK), b * BLK : (b + 1) * BLK] = pan[tab[(tq * 4 + b) * row_blocks + f]]
            return carry

        lax.fori_loop(0, row_blocks, build, 0)
        part = jnp.dot(nxt[...], wide[buf], preferred_element_type=f32)
        if m < nt - 1:
            outb[m] = part.astype(bf16)
            tcopy(m).start()
        else:
            total = part
    for m in range(nt - 1):
        tcopy(m).wait_recv()
        total = total + rcv[m].astype(f32)
    out[...] = total.astype(bf16)

    for m in range(nt - 1):
        tcopy(m).wait_send()
    for q in range(2):
        ycopy(q).wait_send()

    def drain(s, carry):
        for u in range(2):
            for q in range(2):
                dcopy(s, q, u).wait_send()
        return carry

    def drain_ring(s, carry):
        for u in range(2):
            for q in range(2):
                rcopy(s, q, u).wait_send()
        return carry

    lax.fori_loop(0, nz, drain, 0)
    lax.fori_loop(0, nz - 1, drain_ring, 0)


def tables(pattern, owners, dp_devices, slots, row_blocks, col_blocks):
    keep = pattern.shape[1]
    total = row_blocks * keep
    owner = owners.reshape(total)
    number = jnp.arange(total, dtype=jnp.int32)
    same = owner[:, None] == owner[None, :]
    earlier = number[None, :] < number[:, None]
    position = jnp.sum((same & earlier).astype(jnp.int32), axis=1)
    target = owner * slots + position
    where = pattern.reshape(total) * row_blocks + number // keep
    places = jnp.arange(dp_devices * slots, dtype=jnp.int32)
    hit = target[None, :] == places[:, None]
    n_dense = row_blocks * col_blocks
    grad_tab = n_dense + jnp.sum(jnp.where(hit, where[None, :] - n_dense, 0), axis=1)
    spots = jnp.arange(n_dense, dtype=jnp.int32)
    found = where[None, :] == spots[:, None]
    n_pan = dp_devices * slots
    next_tab = n_pan + jnp.sum(jnp.where(found, target[None, :] - n_pan, 0), axis=1)
    people = jnp.arange(dp_devices, dtype=jnp.int32)
    count = jnp.sum((owner[None, :] == people[:, None]).astype(jnp.int32), axis=1)
    return grad_tab, next_tab, count


def per_device(hidden, cotangent, weight_slots, pattern, owners, first_moment, second_moment, next_hidden):
    tokens, width = hidden.shape
    cols = cotangent.shape[1]
    row_blocks = pattern.shape[0]
    slots = first_moment.shape[2]
    n_dp, n_t = lax.axis_size("dp"), lax.axis_size("tensor")
    nz, nx = n_dp // 4, n_t // 2
    col_blocks = cols * n_t // BLK
    hs = slots // 2
    grad_tab, next_tab, count = tables(pattern, owners, n_dp, slots, row_blocks, col_blocks)

    vmem = pl.BlockSpec(memory_space=pltpu.VMEM)
    smem = pl.BlockSpec(memory_space=pltpu.SMEM)
    dma = pltpu.SemaphoreType.DMA
    block = (slots, BLK, BLK)
    new1, new2, panels = pl.pallas_call(
        functools.partial(grad_kernel, nz, nx, slots, row_blocks),
        out_shape=(
            jax.ShapeDtypeStruct(block, f32),
            jax.ShapeDtypeStruct(block, f32),
            jax.ShapeDtypeStruct(block, bf16),
        ),
        in_specs=[smem, smem] + [vmem] * 5,
        out_specs=(vmem, vmem, vmem),
        scratch_shapes=[
            pltpu.VMEM((n_t, tokens, cols), bf16),
            pltpu.VMEM((width, tokens), bf16),
            pltpu.VMEM((row_blocks * col_blocks + 1, BLK, BLK), bf16),
            pltpu.VMEM((nz, 2, 2, hs, BLK, BLK), bf16),
            pltpu.VMEM((nz, 2, 2, hs, BLK, BLK), bf16),
            pltpu.VMEM((nz - 1, 2, 2, hs, BLK, BLK), bf16),
            pltpu.VMEM((2, hs, BLK, BLK), bf16),
            dma((CHUNKS,)),
            dma((CHUNKS,)),
            dma((2, 2, CHUNKS)),
            dma((2, 2, CHUNKS)),
            dma((2, 2, CHUNKS)),
            dma((2, 2, CHUNKS)),
            dma((nz, 2)),
            dma((nz, 2)),
            dma((nz - 1, 2, 2)),
            dma((nz - 1, 2, 2)),
            dma((2,)),
            dma((2,)),
        ],
        compiler_params=pltpu.CompilerParams(
            collective_id=0, has_side_effects=True, vmem_limit_bytes=60 * 1024 * 1024
        ),
        name="grad_adam",
    )(grad_tab, count, hidden, cotangent, weight_slots[0, 0], first_moment[0, 0], second_moment[0, 0])

    next_out = pl.pallas_call(
        functools.partial(next_kernel, nz, nx, slots, row_blocks),
        out_shape=jax.ShapeDtypeStruct((next_hidden.shape[0], cols), bf16),
        in_specs=[smem, vmem, vmem],
        out_specs=vmem,
        scratch_shapes=[
            pltpu.VMEM((n_dp * slots + 1, BLK, BLK), bf16),
            pltpu.VMEM((2, width, cols), bf16),
            pltpu.VMEM((n_t - 1, next_hidden.shape[0], cols), bf16),
            pltpu.VMEM((n_t - 1, next_hidden.shape[0], cols), bf16),
            dma((2,)),
            dma((2,)),
            dma((nz - 1, 2, 2)),
            dma((nz - 1, 2, 2)),
            dma((nz, 2, 2)),
            dma((nz, 2, 2)),
            dma((n_t - 1,)),
            dma((n_t - 1,)),
        ],
        compiler_params=pltpu.CompilerParams(
            collective_id=1, has_side_effects=True, vmem_limit_bytes=60 * 1024 * 1024
        ),
        name="gather_next",
    )(next_tab, panels, next_hidden)
    return next_out, new1[None, None], new2[None, None]


def solution(mesh):
    in_specs = (
        P("dp", "tensor"),
        P("dp", "tensor"),
        P("tensor", "dp", None, None, None),
        P("tensor", None),
        P("tensor", None, None),
        P("tensor", "dp", None, None, None),
        P("tensor", "dp", None, None, None),
        P("dp", "tensor"),
    )
    out_specs = (
        P("dp", "tensor"),
        P("tensor", "dp", None, None, None),
        P("tensor", "dp", None, None, None),
    )
    return jax.shard_map(
        per_device, mesh=mesh, in_specs=in_specs, out_specs=out_specs, check_vma=False
    )
```

```python
import functools

import jax
import jax.numpy as jnp
from jax import lax
from jax.experimental import pallas as pl
from jax.experimental.pallas import tpu as pltpu
from jax.sharding import PartitionSpec as P

ADAM_STEP = 20
BETA_ONE = 0.9
BETA_TWO = 0.95
LEARN_RATE = 0.003
EPSILON = 1e-08

BLK = 128
CHUNKS = 4
ZF = 2
MESH = pl.DeviceIdType.MESH
f32 = jnp.float32
bf16 = jnp.bfloat16


def remote(src, dst, send, recv, where):
    return pltpu.make_async_remote_copy(
        src_ref=src, dst_ref=dst, send_sem=send, recv_sem=recv, device_id=where, device_id_type=MESH
    )


def greet(places):
    barrier = pltpu.get_barrier_semaphore()
    for where in places:
        pl.semaphore_signal(barrier, inc=1, device_id=where, device_id_type=MESH)
    pl.semaphore_wait(barrier, len(places))


class Place:
    def __init__(self, nz, nx):
        self.nz, self.nx = nz, nx
        self.d = lax.axis_index("dp")
        self.t = lax.axis_index("tensor")
        self.z = lax.div(self.d, 4)
        self.yl = lax.rem(lax.div(self.d, 2), 2)
        self.core = lax.rem(self.d, 2)
        self.x = lax.div(self.t, 2)
        self.yh = lax.rem(self.t, 2)

    def dp_of(self, z, yl, core):
        return (z * 2 + yl) * 2 + core

    def tensor_of(self, x, yh):
        return x * 2 + yh

    def x_step(self, k):
        return lax.rem(self.x + (k + self.nx), self.nx)

    def z_step(self, k):
        return lax.rem(self.z + (k + self.nz), self.nz)


def grad_kernel(
    nz, nx, slots, row_blocks,
    tab, cnt, hid, cot, wgt, m1, m2,
    new1, new2, panels,
    cotbuf, dense, acc, sendb, recvb, ringb, ybuf, yrecv,
    ys, yr, xs, xr, fs, fr, os, orr, ds, dr, rs, rr, ps, pr, ls, lr,
):
    me = Place(nz, nx)
    tokens = cot.shape[0]
    rows = tokens // CHUNKS
    half = rows // 2
    early = tokens // 2
    n_dense = dense.shape[0] - 1
    hs = slots // 2

    y_far = {"tensor": me.tensor_of(me.x, 1 - me.yh)}
    x_next = [{"tensor": me.tensor_of(me.x_step(1), me.yh)}, {"tensor": me.tensor_of(me.x_step(-1), me.yh)}]
    z_next = [{"dp": me.dp_of(me.z_step(1), me.yl, me.core)}, {"dp": me.dp_of(me.z_step(-1), me.yl, me.core)}]
    y_near = {"dp": me.dp_of(me.z, 1 - me.yl, me.core)}
    twin = {"dp": me.dp_of(me.z, me.yl, 1 - me.core)}
    greet([y_far] + x_next + z_next + [y_near, twin])

    t_item = [me.t, me.tensor_of(me.x, 1 - me.yh)]
    x_opp = me.x_step(2)
    t_opp = [me.tensor_of(x_opp, me.yh), me.tensor_of(x_opp, 1 - me.yh)]

    def t_from(item, q):
        yh = me.yh if item == 0 else 1 - me.yh
        return me.tensor_of(me.x_step(-1 if q == 0 else 1), yh)

    def ycopy(c):
        r = pl.ds(c * rows, rows)
        return remote(cot.at[r], cotbuf.at[me.t, r], ys.at[c], yr.at[c], y_far)

    def xcopy(item, q, c):
        r = pl.ds(c * rows, rows)
        src = cot.at[r] if item == 0 else cotbuf.at[t_item[1], r]
        return remote(src, cotbuf.at[t_item[item], r], xs.at[item, q, c], xr.at[item, q, c], x_next[q])

    def fcopy(q, c):
        r = pl.ds(c * rows + q * half, half)
        there = cotbuf.at[t_from(0, q), r]
        return remote(there, there, fs.at[q, c], fr.at[q, c], x_next[q])

    def ocopy(q, c):
        r = pl.ds(c * rows + q * half, half)
        there = cotbuf.at[t_opp[0], r]
        return remote(there, there, os.at[q, c], orr.at[q, c], y_far)

    def group(src, tq, lo=0, hi=tokens, keep=None, plus=None):
        for i in range(row_blocks // 2):
            wide = slice(i * 256, (i + 1) * 256)
            out = lax.dot_general(
                hid[lo:hi, wide], src[lo:hi, :], (((0,), (0,)), ((), ())), preferred_element_type=f32
            )
            if plus is not None:
                out = out + acc[plus, wide, :]
            if keep is not None:
                acc[keep, wide, :] = out
                continue
            for b in range(4):
                for a in range(2):
                    dense[(tq * 4 + b) * row_blocks + 2 * i + a] = out[
                        a * BLK : (a + 1) * BLK, b * BLK : (b + 1) * BLK
                    ].astype(bf16)

    queue = [functools.partial(xcopy, 0, c=0), functools.partial(xcopy, 0, c=1)]
    for c in range(CHUNKS):
        queue.append(functools.partial(fcopy, c=c))
        if c + 2 < CHUNKS:
            queue.append(functools.partial(xcopy, 0, c=c + 2))
        if c == CHUNKS - 2:
            queue.append(functools.partial(xcopy, 1, c=0))
    queue += [functools.partial(xcopy, 1, c=c) for c in range(1, CHUNKS)]

    def go(k):
        for q in range(2):
            queue[k](q=q).start()

    def got(k):
        for q in range(2):
            queue[k](q=q).wait_recv()
        if k + 2 < len(queue):
            go(k + 2)

    def across(c):
        for q in range(2):
            ocopy(q, c).start()

    go(0)
    ycopy(0).start()
    go(1)
    ycopy(1).start()
    dense[n_dense] = jnp.zeros((BLK, BLK), bf16)
    group(cot, me.t)
    got(0)
    ycopy(0).wait_recv()
    ycopy(2).start()
    got(1)
    ycopy(1).wait_recv()
    got(2)
    across(0)
    got(3)
    ycopy(2).wait_recv()
    ycopy(3).start()
    got(4)
    across(1)
    got(5)
    group(cotbuf.at[t_from(0, 0)], t_from(0, 0))
    got(6)
    across(2)
    group(cotbuf.at[t_from(0, 1)], t_from(0, 1))
    ycopy(3).wait_recv()
    got(7)
    group(cotbuf.at[t_item[1]], t_item[1])
    got(8)
    across(3)
    group(cotbuf.at[t_opp[0]], t_opp[0])
    got(9)
    for q in range(2):
        group(cotbuf.at[t_from(1, q)], None, hi=early, keep=q)
    for q in range(2):
        for c in range(CHUNKS):
            ocopy(q, c).wait_recv()
    got(10)
    group(cotbuf.at[t_opp[1]], t_opp[1])
    got(11)
    for q in range(2):
        group(cotbuf.at[t_from(1, q)], t_from(1, q), lo=early, plus=q)

    yf = hs - ZF
    order = [(0, i) for i in range(ZF, hs)] + [(0, i) for i in range(ZF)] + [(1, i) for i in range(hs)]
    part = [(yf, hs), (hs, hs + ZF), (hs + ZF, 2 * hs)]

    def dest_z(s, q):
        return lax.rem(me.z + (2 * nz - 1 - s), nz) if q == 0 else lax.rem(me.z + 1 + s, nz)

    def pick(s, q, p, core):
        u, i = order[p]
        yl = 1 - me.yl if u == 0 else me.yl
        return dense[tab[me.dp_of(dest_z(s, q), yl, core) * slots + q * hs + i]]

    def dcopy(s, q):
        return remote(sendb.at[s, q], recvb.at[s, q], ds.at[s, q], dr.at[s, q], twin)

    def pcopy(s, q):
        return remote(recvb.at[s, q, pl.ds(0, yf)], ybuf.at[s, q], ps.at[s, q], pr.at[s, q], y_near)

    def rcopy(s, q, n):
        lo, hi = part[n]
        return remote(
            recvb.at[s, q, pl.ds(lo, hi - lo)], ringb.at[s, q, pl.ds(lo - yf, hi - lo)],
            rs.at[s, q, n], rr.at[s, q, n], z_next[q],
        )

    def lcopy(q):
        return remote(recvb.at[nz - 1, q, pl.ds(yf, ZF)], yrecv.at[q], ls.at[q], lr.at[q], y_near)

    def fill(s):
        for q in range(2):
            for p in range(2 * hs):
                sendb[s, q, p] = pick(s, q, p, 1 - me.core)
            dcopy(s, q).start()

    def spread(s):
        for q in range(2):
            dcopy(s, q).wait_recv()
            for p in range(yf):
                recvb[s, q, p] = (recvb[s, q, p].astype(f32) + pick(s, q, p, me.core).astype(f32)).astype(bf16)
            pcopy(s, q).start()

    def add(s, q, n, first):
        lo, hi = part[n]
        for p in range(lo, hi):
            v = recvb[s, q, p].astype(f32) + pick(s, q, p, me.core).astype(f32)
            if n == 2:
                v = v + ybuf[s, q, p - lo].astype(f32)
            if not first:
                v = v + ringb[s - 1, q, p - yf].astype(f32)
            recvb[s, q, p] = v.astype(bf16)

    fill(0)
    fill(1)
    spread(0)
    fill(2)
    for n in range(2):
        for q in range(2):
            add(0, q, n, True)
            rcopy(0, q, n).start()
    spread(1)
    fill(3)
    for q in range(2):
        pcopy(0, q).wait_recv()
        add(0, q, 2, True)
        rcopy(0, q, 2).start()

    def hop(s):
        for n in range(3):
            for q in range(2):
                rcopy(s - 1, q, n).wait_recv()
                if n == 2:
                    pcopy(s, q).wait_recv()
                add(s, q, n, False)
                rcopy(s, q, n).start()

    def ring(s, carry):
        spread(s + 1)
        fill(s + 3)
        hop(s)
        return carry

    lax.fori_loop(1, nz - 3, ring, 0)
    for s in range(nz - 3, nz - 1):
        spread(s + 1)
        hop(s)
    for n in range(3):
        for q in range(2):
            rcopy(nz - 2, q, n).wait_recv()
            if n == 2:
                pcopy(nz - 1, q).wait_recv()
            add(nz - 1, q, n, False)
            if n == 0:
                lcopy(q).start()

    scale_one = 1.0 - BETA_ONE**ADAM_STEP
    scale_two = 1.0 - BETA_TWO**ADAM_STEP
    mine = cnt[me.d]

    def adam(q, i):
        k = q * hs + i
        grad = recvb[nz - 1, q, hs + i].astype(f32)
        if i < ZF:
            grad = grad + yrecv[q, i].astype(f32)
        used = k < mine
        one = jnp.where(used, BETA_ONE * m1[k] + (1 - BETA_ONE) * grad, 0.0)
        two = jnp.where(used, BETA_TWO * m2[k] + (1 - BETA_TWO) * grad * grad, 0.0)
        new1[k] = one
        new2[k] = two
        step = LEARN_RATE * (one / scale_one) / (jnp.sqrt(two / scale_two) + EPSILON)
        panels[k] = (wgt[k].astype(f32) - step).astype(bf16)

    for q in range(2):
        for i in range(ZF, hs):
            adam(q, i)
    for q in range(2):
        lcopy(q).wait_recv()
        for i in range(ZF):
            adam(q, i)

    for c in range(CHUNKS):
        ycopy(c).wait_send()
        for q in range(2):
            for item in range(2):
                xcopy(item, q, c).wait_send()
            fcopy(q, c).wait_send()
            ocopy(q, c).wait_send()
    for q in range(2):
        lcopy(q).wait_send()

    def drain(s, carry):
        for q in range(2):
            dcopy(s, q).wait_send()
            pcopy(s, q).wait_send()
        return carry

    def drain_ring(s, carry):
        for q in range(2):
            for n in range(3):
                rcopy(s, q, n).wait_send()
        return carry

    lax.fori_loop(0, nz, drain, 0)
    lax.fori_loop(0, nz - 1, drain_ring, 0)


def next_kernel(
    nz, nx, slots, row_blocks,
    tab, panel, nxt,
    out,
    pan, wide, outb, rcv,
    ys, yr, ps, pr, rs, rr, ds, dr, es, er, ts, tr,
):
    me = Place(nz, nx)
    nt = 2 * nx
    hs = slots // 2
    n_pan = nz * 4 * slots

    z_next = [{"dp": me.dp_of(me.z_step(1), me.yl, me.core)}, {"dp": me.dp_of(me.z_step(-1), me.yl, me.core)}]
    y_near = {"dp": me.dp_of(me.z, 1 - me.yl, me.core)}
    twin = {"dp": me.dp_of(me.z, me.yl, 1 - me.core)}
    peers = [{"tensor": lax.rem(me.t + 1 + m, nt)} for m in range(nt - 1)]
    greet(z_next + [y_near, twin] + peers)

    def place(s, q, u, lo, n):
        z = lax.rem(me.z + (2 * nz - s), nz) if q == 0 else lax.rem(me.z + s, nz)
        yl = me.yl if u == 0 else 1 - me.yl
        return pan.at[pl.ds(me.dp_of(z, yl, me.core) * slots + q * hs + lo, n)]

    def ycopy(q):
        return remote(panel.at[pl.ds(q * hs, ZF)], place(0, q, 0, 0, ZF), ys.at[q], yr.at[q], y_near)

    def pcopy(s, q):
        here = place(s, q, 0, ZF, hs - ZF)
        return remote(here, here, ps.at[s, q], pr.at[s, q], y_near)

    pieces = [(0, 0, ZF), (0, ZF, hs - ZF), (1, 0, ZF)]

    def rcopy(s, q, n):
        here = place(s, q, *pieces[n])
        return remote(here, here, rs.at[s, q, n], rr.at[s, q, n], z_next[q])

    def dcopy(s, q, u):
        here = place(s, q, u, 0, hs if u == 0 else ZF)
        return remote(here, here, ds.at[s, q, u], dr.at[s, q, u], twin)

    def ecopy(s, q):
        here = place(s, q, 1, ZF, hs - ZF)
        return remote(here, here, es.at[s, q], er.at[s, q], twin)

    for q in range(2):
        ycopy(q).start()
    for i in range(slots):
        pan[me.d * slots + i] = panel[i]
    for n in range(2):
        for q in range(2):
            rcopy(0, q, n).start()
    for q in range(2):
        pcopy(0, q).start()
        dcopy(0, q, 0).start()
    pan[n_pan] = jnp.zeros((BLK, BLK), bf16)
    for q in range(2):
        ycopy(q).wait_recv()
        rcopy(0, q, 2).start()
        dcopy(0, q, 1).start()

    def hop(s, last):
        for q in range(2):
            rcopy(s - 1, q, 1).wait_recv()
            if not last:
                rcopy(s, q, 1).start()
            pcopy(s, q).start()
        for q in range(2):
            rcopy(s - 1, q, 0).wait_recv()
            if not last:
                rcopy(s, q, 0).start()
            dcopy(s, q, 0).start()
        for q in range(2):
            rcopy(s - 1, q, 2).wait_recv()
            if not last:
                rcopy(s, q, 2).start()
            dcopy(s, q, 1).start()
        for q in range(2):
            pcopy(s - 1, q).wait_recv()
            ecopy(s - 1, q).start()

    def ring(s, carry):
        hop(s, False)
        return carry

    lax.fori_loop(1, nz - 1, ring, 0)
    hop(nz - 1, True)
    for q in range(2):
        pcopy(nz - 1, q).wait_recv()
        ecopy(nz - 1, q).start()

    def landed(s, carry):
        for q in range(2):
            dcopy(s, q, 0).wait_recv()
            dcopy(s, q, 1).wait_recv()
            ecopy(s, q).wait_recv()
        return carry

    lax.fori_loop(0, nz, landed, 0)

    def tcopy(m):
        return remote(outb.at[m], rcv.at[m], ts.at[m], tr.at[m], peers[m])

    total = None
    for m in range(nt):
        tq = lax.rem(me.t + 1 + m, nt)
        buf = m % 2

        def build(h, carry):
            for b in range(4):
                for i in range(row_blocks // 2):
                    f = h * (row_blocks // 2) + i
                    wide[buf, pl.ds(f * BLK, BLK), b * BLK : (b + 1) * BLK] = pan[tab[(tq * 4 + b) * row_blocks + f]]
            return carry

        lax.fori_loop(0, 2, build, 0)
        part = jnp.dot(nxt[...], wide[buf], preferred_element_type=f32)
        if m < nt - 1:
            outb[m] = part.astype(bf16)
            tcopy(m).start()
        else:
            total = part
    for m in range(nt - 1):
        tcopy(m).wait_recv()
        total = total + rcv[m].astype(f32)
    out[...] = total.astype(bf16)

    for m in range(nt - 1):
        tcopy(m).wait_send()
    for q in range(2):
        ycopy(q).wait_send()

    def drain(s, carry):
        for u in range(2):
            for q in range(2):
                dcopy(s, q, u).wait_send()
        for q in range(2):
            pcopy(s, q).wait_send()
            ecopy(s, q).wait_send()
        return carry

    def drain_ring(s, carry):
        for n in range(3):
            for q in range(2):
                rcopy(s, q, n).wait_send()
        return carry

    lax.fori_loop(0, nz, drain, 0)
    lax.fori_loop(0, nz - 1, drain_ring, 0)


def tables(pattern, owners, dp_devices, slots, row_blocks, col_blocks):
    keep = pattern.shape[1]
    total = row_blocks * keep
    owner = owners.reshape(total)
    number = jnp.arange(total, dtype=jnp.int32)
    same = owner[:, None] == owner[None, :]
    earlier = number[None, :] < number[:, None]
    position = jnp.sum((same & earlier).astype(jnp.int32), axis=1)
    target = owner * slots + position
    where = pattern.reshape(total) * row_blocks + number // keep
    places = jnp.arange(dp_devices * slots, dtype=jnp.int32)
    hit = target[None, :] == places[:, None]
    n_dense = row_blocks * col_blocks
    grad_tab = n_dense + jnp.sum(jnp.where(hit, where[None, :] - n_dense, 0), axis=1)
    spots = jnp.arange(n_dense, dtype=jnp.int32)
    found = where[None, :] == spots[:, None]
    n_pan = dp_devices * slots
    next_tab = n_pan + jnp.sum(jnp.where(found, target[None, :] - n_pan, 0), axis=1)
    people = jnp.arange(dp_devices, dtype=jnp.int32)
    count = jnp.sum((owner[None, :] == people[:, None]).astype(jnp.int32), axis=1)
    return grad_tab, next_tab, count


def per_device(hidden, cotangent, weight_slots, pattern, owners, first_moment, second_moment, next_hidden):
    tokens, width = hidden.shape
    cols = cotangent.shape[1]
    row_blocks = pattern.shape[0]
    slots = first_moment.shape[2]
    n_dp, n_t = lax.axis_size("dp"), lax.axis_size("tensor")
    nz, nx = n_dp // 4, n_t // 2
    col_blocks = cols * n_t // BLK
    hs = slots // 2
    grad_tab, next_tab, count = tables(pattern, owners, n_dp, slots, row_blocks, col_blocks)

    vmem = pl.BlockSpec(memory_space=pltpu.VMEM)
    smem = pl.BlockSpec(memory_space=pltpu.SMEM)
    dma = pltpu.SemaphoreType.DMA
    block = (slots, BLK, BLK)
    new1, new2, panels = pl.pallas_call(
        functools.partial(grad_kernel, nz, nx, slots, row_blocks),
        out_shape=(
            jax.ShapeDtypeStruct(block, f32),
            jax.ShapeDtypeStruct(block, f32),
            jax.ShapeDtypeStruct(block, bf16),
        ),
        in_specs=[smem, smem] + [vmem] * 5,
        out_specs=(vmem, vmem, vmem),
        scratch_shapes=[
            pltpu.VMEM((n_t, tokens, cols), bf16),
            pltpu.VMEM((row_blocks * col_blocks + 1, BLK, BLK), bf16),
            pltpu.VMEM((2, width, cols), f32),
            pltpu.VMEM((nz, 2, slots, BLK, BLK), bf16),
            pltpu.VMEM((nz, 2, slots, BLK, BLK), bf16),
            pltpu.VMEM((nz - 1, 2, hs + ZF, BLK, BLK), bf16),
            pltpu.VMEM((nz, 2, hs - ZF, BLK, BLK), bf16),
            pltpu.VMEM((2, ZF, BLK, BLK), bf16),
            dma((CHUNKS,)),
            dma((CHUNKS,)),
            dma((2, 2, CHUNKS)),
            dma((2, 2, CHUNKS)),
            dma((2, CHUNKS)),
            dma((2, CHUNKS)),
            dma((2, CHUNKS)),
            dma((2, CHUNKS)),
            dma((nz, 2)),
            dma((nz, 2)),
            dma((nz - 1, 2, 3)),
            dma((nz - 1, 2, 3)),
            dma((nz, 2)),
            dma((nz, 2)),
            dma((2,)),
            dma((2,)),
        ],
        compiler_params=pltpu.CompilerParams(
            collective_id=0, has_side_effects=True, vmem_limit_bytes=60 * 1024 * 1024
        ),
        name="grad_adam",
    )(grad_tab, count, hidden, cotangent, weight_slots[0, 0], first_moment[0, 0], second_moment[0, 0])

    next_out = pl.pallas_call(
        functools.partial(next_kernel, nz, nx, slots, row_blocks),
        out_shape=jax.ShapeDtypeStruct((next_hidden.shape[0], cols), bf16),
        in_specs=[smem, vmem, vmem],
        out_specs=vmem,
        scratch_shapes=[
            pltpu.VMEM((n_dp * slots + 1, BLK, BLK), bf16),
            pltpu.VMEM((2, width, cols), bf16),
            pltpu.VMEM((n_t - 1, next_hidden.shape[0], cols), bf16),
            pltpu.VMEM((n_t - 1, next_hidden.shape[0], cols), bf16),
            dma((2,)),
            dma((2,)),
            dma((nz, 2)),
            dma((nz, 2)),
            dma((nz - 1, 2, 3)),
            dma((nz - 1, 2, 3)),
            dma((nz, 2, 2)),
            dma((nz, 2, 2)),
            dma((nz, 2)),
            dma((nz, 2)),
            dma((n_t - 1,)),
            dma((n_t - 1,)),
        ],
        compiler_params=pltpu.CompilerParams(
            collective_id=1, has_side_effects=True, vmem_limit_bytes=60 * 1024 * 1024
        ),
        name="gather_next",
    )(next_tab, panels, next_hidden)
    return next_out, new1[None, None], new2[None, None]


def solution(mesh):
    in_specs = (
        P("dp", "tensor"),
        P("dp", "tensor"),
        P("tensor", "dp", None, None, None),
        P("tensor", None),
        P("tensor", None, None),
        P("tensor", "dp", None, None, None),
        P("tensor", "dp", None, None, None),
        P("dp", "tensor"),
    )
    out_specs = (
        P("dp", "tensor"),
        P("tensor", "dp", None, None, None),
        P("tensor", "dp", None, None, None),
    )
    return jax.shard_map(
        per_device, mesh=mesh, in_specs=in_specs, out_specs=out_specs, check_vma=False
    )
```

```python
import functools

import jax
import jax.numpy as jnp
from jax import lax
from jax.experimental import pallas as pl
from jax.experimental.pallas import tpu as pltpu
from jax.sharding import PartitionSpec as P

ADAM_STEP = 20
BETA_ONE = 0.9
BETA_TWO = 0.95
LEARN_RATE = 0.003
EPSILON = 1e-08

BLK = 128
CHUNKS = 4

ZF = 2
MESH = pl.DeviceIdType.MESH
f32 = jnp.float32
bf16 = jnp.bfloat16


def remote(src, dst, send, recv, where):
    return pltpu.make_async_remote_copy(
        src_ref=src, dst_ref=dst, send_sem=send, recv_sem=recv, device_id=where, device_id_type=MESH
    )


def greet(places):
    barrier = pltpu.get_barrier_semaphore()
    for where in places:
        pl.semaphore_signal(barrier, inc=1, device_id=where, device_id_type=MESH)
    pl.semaphore_wait(barrier, len(places))


class Place:
    def __init__(self, nz, nx):
        self.nz, self.nx = nz, nx
        self.d = lax.axis_index("dp")
        self.t = lax.axis_index("tensor")
        self.z = lax.div(self.d, 4)
        self.yl = lax.rem(lax.div(self.d, 2), 2)
        self.core = lax.rem(self.d, 2)
        self.x = lax.div(self.t, 2)
        self.yh = lax.rem(self.t, 2)

    def dp_of(self, z, yl, core):
        return (z * 2 + yl) * 2 + core

    def tensor_of(self, x, yh):
        return x * 2 + yh

    def x_step(self, k):
        return lax.rem(self.x + (k + self.nx), self.nx)

    def z_step(self, k):
        return lax.rem(self.z + (k + self.nz), self.nz)


def moments(grad, used, one, two):
    one = jnp.where(used, BETA_ONE * one + (1 - BETA_ONE) * grad, 0.0)
    two = jnp.where(used, BETA_TWO * two + (1 - BETA_TWO) * grad * grad, 0.0)
    return one, two


def kernel(
    nz, nx, slots, row_blocks,
    tab, cot, hid_in, wgt_in, m1_in, m2_in, nxt_in,
    out, grads,
    hid, wgt, m1, m2, nxt,
    cotbuf, dense, acc, sendb, recvb, ringb, ybuf, yrecv, outb, rcv,
    ins, free,
    ys, yr, xs, xr, fs, fr, os, orr,
    ds, dr, rs, rr, ps, pr, ls, lr,
    ys2, yr2, ps2, pr2, rs2, rr2, ds2, dr2, es, er, ts, tr,
):
    me = Place(nz, nx)
    nt = 2 * nx
    tokens = cot.shape[0]
    width = hid.shape[1]
    rows = tokens // CHUNKS
    half = rows // 2
    early = tokens // 2
    n_dense = dense.shape[0] - 1
    n_slots = nz * 4 * slots
    hs = slots // 2

    loads = [
        pltpu.make_async_copy(src, dst, ins.at[i])
        for i, (src, dst) in enumerate([(hid_in, hid), (wgt_in, wgt), (m1_in, m1), (m2_in, m2), (nxt_in, nxt)])
    ]
    for load in loads:
        load.start()

    y_far = {"tensor": me.tensor_of(me.x, 1 - me.yh)}
    x_next = [{"tensor": me.tensor_of(me.x_step(1), me.yh)}, {"tensor": me.tensor_of(me.x_step(-1), me.yh)}]
    z_next = [{"dp": me.dp_of(me.z_step(1), me.yl, me.core)}, {"dp": me.dp_of(me.z_step(-1), me.yl, me.core)}]
    y_near = {"dp": me.dp_of(me.z, 1 - me.yl, me.core)}
    twin = {"dp": me.dp_of(me.z, me.yl, 1 - me.core)}
    near = z_next + [y_near, twin]
    away = [(2, 1), (1, 1), (nx - 1, 1), (0, 1), (2, 0), (1, 0), (nx - 1, 0)]
    t_away = [me.tensor_of(me.x_step(dx), 1 - me.yh if far else me.yh) for dx, far in away] + [me.t]
    peers = [{"tensor": t_away[m]} for m in range(nt - 1)]
    greet(near + peers)

    t_item = [me.t, me.tensor_of(me.x, 1 - me.yh)]
    x_opp = me.x_step(2)
    t_opp = [me.tensor_of(x_opp, me.yh), me.tensor_of(x_opp, 1 - me.yh)]

    def t_from(item, q):
        yh = me.yh if item == 0 else 1 - me.yh
        return me.tensor_of(me.x_step(-1 if q == 0 else 1), yh)

    def held(t, lo, n):
        return cotbuf.at[pl.ds(t * tokens + lo, n)]

    def ycopy(c):
        return remote(cot.at[pl.ds(c * rows, rows)], held(me.t, c * rows, rows), ys.at[c], yr.at[c], y_far)

    def xcopy(item, q, c):
        there = held(t_item[item], c * rows, rows)
        src = cot.at[pl.ds(c * rows, rows)] if item == 0 else there
        return remote(src, there, xs.at[item, q, c], xr.at[item, q, c], x_next[q])

    def fcopy(q, c):
        there = held(t_from(0, q), c * rows + q * half, half)
        return remote(there, there, fs.at[q, c], fr.at[q, c], x_next[q])

    def ocopy(q, c):
        there = held(t_opp[0], c * rows + q * half, half)
        return remote(there, there, os.at[q, c], orr.at[q, c], y_far)

    def group(src, tq, lo=0, hi=tokens, keep=None, plus=None):
        for i in range(row_blocks // 2):
            wide = slice(i * 256, (i + 1) * 256)
            got_here = lax.dot_general(
                hid[lo:hi, wide], src[lo:hi, :], (((0,), (0,)), ((), ())), preferred_element_type=f32
            )
            if plus is not None:
                got_here = got_here + acc[plus, wide, :]
            if keep is not None:
                acc[keep, wide, :] = got_here
                continue
            for b in range(4):
                for a in range(2):
                    dense[(tq * 4 + b) * row_blocks + 2 * i + a] = got_here[
                        a * BLK : (a + 1) * BLK, b * BLK : (b + 1) * BLK
                    ].astype(bf16)

    def group_of(t, **how):
        group(held(t, 0, tokens), t, **how)

    queue = [functools.partial(xcopy, 0, c=0), functools.partial(xcopy, 0, c=1)]
    for c in range(CHUNKS):
        queue.append(functools.partial(fcopy, c=c))
        if c + 2 < CHUNKS:
            queue.append(functools.partial(xcopy, 0, c=c + 2))
        if c == CHUNKS - 2:
            queue.append(functools.partial(xcopy, 1, c=0))
    queue += [functools.partial(xcopy, 1, c=c) for c in range(1, CHUNKS)]

    def go(k):
        for q in range(2):
            queue[k](q=q).start()

    def got(k):
        for q in range(2):
            queue[k](q=q).wait_recv()
        if k + 2 < len(queue):
            go(k + 2)

    def across(c):
        for q in range(2):
            ocopy(q, c).start()

    go(0)
    ycopy(0).start()
    go(1)
    ycopy(1).start()
    dense[n_dense] = jnp.zeros((BLK, BLK), bf16)
    loads[0].wait()
    group(cot, me.t)
    got(0)
    ycopy(0).wait_recv()
    ycopy(2).start()
    got(1)
    ycopy(1).wait_recv()
    got(2)
    across(0)
    got(3)
    ycopy(2).wait_recv()
    ycopy(3).start()
    got(4)
    across(1)
    got(5)
    group_of(t_from(0, 0))
    got(6)
    across(2)
    group_of(t_from(0, 1))
    ycopy(3).wait_recv()
    got(7)
    group_of(t_item[1])
    got(8)
    across(3)
    group_of(t_opp[0])
    got(9)
    for q in range(2):
        group_of(t_from(1, q), hi=early, keep=q)
    for q in range(2):
        for c in range(CHUNKS):
            ocopy(q, c).wait_recv()
    got(10)
    group_of(t_opp[1])
    got(11)
    for q in range(2):
        group_of(t_from(1, q), lo=early, plus=q)

    yf = hs - ZF
    order = [(0, i) for i in range(ZF, hs)] + [(0, i) for i in range(ZF)] + [(1, i) for i in range(hs)]
    part = [(yf, hs), (hs, hs + ZF), (hs + ZF, 2 * hs)]

    def dest_z(s, q):
        return lax.rem(me.z + (2 * nz - 1 - s), nz) if q == 0 else lax.rem(me.z + 1 + s, nz)

    def pick(s, q, p, core):
        u, i = order[p]
        yl = 1 - me.yl if u == 0 else me.yl
        return dense[tab[me.dp_of(dest_z(s, q), yl, core) * slots + q * hs + i]]

    def dcopy(s, q):
        return remote(sendb.at[s, q], recvb.at[s, q], ds.at[s, q], dr.at[s, q], twin)

    def pcopy(s, q):
        return remote(recvb.at[s, q, pl.ds(0, yf)], ybuf.at[s, q], ps.at[s, q], pr.at[s, q], y_near)

    def rcopy(s, q, n):
        lo, hi = part[n]
        return remote(
            recvb.at[s, q, pl.ds(lo, hi - lo)], ringb.at[s, q, pl.ds(lo - yf, hi - lo)],
            rs.at[s, q, n], rr.at[s, q, n], z_next[q],
        )

    def lcopy(q):
        return remote(recvb.at[nz - 1, q, pl.ds(yf, ZF)], yrecv.at[q], ls.at[q], lr.at[q], y_near)

    def fill(s):
        for q in range(2):
            for p in range(2 * hs):
                sendb[s, q, p] = pick(s, q, p, 1 - me.core)
            dcopy(s, q).start()

    def spread(s):
        for q in range(2):
            dcopy(s, q).wait_recv()
            for p in range(yf):
                recvb[s, q, p] = (recvb[s, q, p].astype(f32) + pick(s, q, p, me.core).astype(f32)).astype(bf16)
            pcopy(s, q).start()

    def add(s, q, n, first=False):
        lo, hi = part[n]
        for p in range(lo, hi):
            v = recvb[s, q, p].astype(f32) + pick(s, q, p, me.core).astype(f32)
            if n == 2:
                v = v + ybuf[s, q, p - lo].astype(f32)
            if not first:
                v = v + ringb[s - 1, q, p - yf].astype(f32)
            recvb[s, q, p] = v.astype(bf16)

    def hop_ahead(s):
        for n in range(2):
            for q in range(2):
                rcopy(s - 1, q, n).wait_recv()
                add(s, q, n)
                rcopy(s, q, n).start()

    def hop_behind(s):
        for q in range(2):
            rcopy(s - 1, q, 2).wait_recv()
            pcopy(s, q).wait_recv()
            add(s, q, 2)
            rcopy(s, q, 2).start()

    fill(0)
    fill(1)
    spread(0)
    fill(2)
    for n in range(2):
        for q in range(2):
            add(0, q, n, True)
            rcopy(0, q, n).start()
    spread(1)
    fill(3)
    hop_ahead(1)
    for q in range(2):
        pcopy(0, q).wait_recv()
        add(0, q, 2, True)
        rcopy(0, q, 2).start()

    def ring(s, carry):
        spread(s)
        fill(s + 2)
        hop_ahead(s)
        hop_behind(s - 1)
        return carry

    lax.fori_loop(2, nz - 2, ring, 0)
    spread(nz - 2)
    hop_ahead(nz - 2)
    hop_behind(nz - 3)
    spread(nz - 1)
    for n in range(2):
        for q in range(2):
            rcopy(nz - 2, q, n).wait_recv()
            add(nz - 1, q, n)
            if n == 0:
                lcopy(q).start()
    hop_behind(nz - 2)
    for q in range(2):
        rcopy(nz - 2, q, 2).wait_recv()
        pcopy(nz - 1, q).wait_recv()
        add(nz - 1, q, 2)

    for where in near:
        pl.semaphore_signal(free, inc=1, device_id=where, device_id_type=MESH)

    pan = dense
    scale_one = 1.0 - BETA_ONE**ADAM_STEP
    scale_two = 1.0 - BETA_TWO**ADAM_STEP
    mine = tab[n_slots + n_dense]
    for load in loads[1:]:
        load.wait()

    def adam(q, i):
        k = q * hs + i
        grad = recvb[nz - 1, q, hs + i].astype(f32)
        if i < ZF:
            grad = grad + yrecv[q, i].astype(f32)
        grads[k] = grad
        one, two = moments(grad, k < mine, m1[k], m2[k])
        step = LEARN_RATE * (one / scale_one) / (jnp.sqrt(two / scale_two) + EPSILON)
        pan[me.d * slots + k] = (wgt[k].astype(f32) - step).astype(bf16)

    for q in range(2):
        for i in range(ZF, hs):
            adam(q, i)
    pl.semaphore_wait(free, len(near))

    def place(s, q, u, lo, n):
        z = lax.rem(me.z + (2 * nz - s), nz) if q == 0 else lax.rem(me.z + s, nz)
        yl = me.yl if u == 0 else 1 - me.yl
        return pan.at[pl.ds(me.dp_of(z, yl, me.core) * slots + q * hs + lo, n)]

    pieces = [(0, 0, ZF), (0, ZF, hs - ZF), (1, 0, ZF)]

    def ycopy2(q):
        here = place(0, q, 0, 0, ZF)
        return remote(here, here, ys2.at[q], yr2.at[q], y_near)

    def pcopy2(s, q):
        here = place(s, q, 0, ZF, hs - ZF)
        return remote(here, here, ps2.at[s, q], pr2.at[s, q], y_near)

    def rcopy2(s, q, n):
        here = place(s, q, *pieces[n])
        return remote(here, here, rs2.at[s, q, n], rr2.at[s, q, n], z_next[q])

    def dcopy2(s, q, u):
        here = place(s, q, u, 0, hs if u == 0 else ZF)
        return remote(here, here, ds2.at[s, q, u], dr2.at[s, q, u], twin)

    def ecopy2(s, q):
        here = place(s, q, 1, ZF, hs - ZF)
        return remote(here, here, es.at[s, q], er.at[s, q], twin)

    for q in range(2):
        rcopy2(0, q, 1).start()
        pcopy2(0, q).start()
    for q in range(2):
        lcopy(q).wait_recv()
        for i in range(ZF):
            adam(q, i)
        ycopy2(q).start()
        rcopy2(0, q, 0).start()
        dcopy2(0, q, 0).start()

    def ahead2(s, last=False):
        for q in range(2):
            rcopy2(s - 1, q, 1).wait_recv()
            if not last:
                rcopy2(s, q, 1).start()
            pcopy2(s, q).start()

    def behind2(s, last=False):
        for n, u in ((0, 0), (2, 1)):
            for q in range(2):
                rcopy2(s - 1, q, n).wait_recv()
                if not last:
                    rcopy2(s, q, n).start()
                dcopy2(s, q, u).start()

    def landed2(s):
        for q in range(2):
            pcopy2(s, q).wait_recv()
            ecopy2(s, q).start()

    ahead2(1)
    for q in range(2):
        ycopy2(q).wait_recv()
        rcopy2(0, q, 2).start()
        dcopy2(0, q, 1).start()
    landed2(0)

    def ring2(s, carry):
        ahead2(s)
        behind2(s - 1)
        landed2(s - 1)
        return carry

    lax.fori_loop(2, nz - 1, ring2, 0)
    ahead2(nz - 1, True)
    behind2(nz - 2)
    landed2(nz - 2)

    for c in range(CHUNKS):
        ycopy(c).wait_send()
        for q in range(2):
            for item in range(2):
                xcopy(item, q, c).wait_send()
            fcopy(q, c).wait_send()
            ocopy(q, c).wait_send()

    behind2(nz - 1, True)
    landed2(nz - 1)

    def all_here(s, carry):
        for q in range(2):
            dcopy2(s, q, 0).wait_recv()
            dcopy2(s, q, 1).wait_recv()
            ecopy2(s, q).wait_recv()
        return carry

    lax.fori_loop(0, nz, all_here, 0)

    def tcopy(m):
        return remote(outb.at[m], rcv.at[m], ts.at[m], tr.at[m], peers[m])

    total = None
    for m in range(nt):
        tq = t_away[m]
        lo = (m % 2) * width

        def build(h, carry):
            for b in range(4):
                for i in range(row_blocks // 2):
                    f = h * (row_blocks // 2) + i
                    cotbuf[pl.ds(lo + f * BLK, BLK), b * BLK : (b + 1) * BLK] = pan[tab[n_slots + (tq * 4 + b) * row_blocks + f]]
            return carry

        lax.fori_loop(0, 2, build, 0)
        piece = jnp.dot(nxt[...], cotbuf[lo : lo + width, :], preferred_element_type=f32)
        if m < nt - 1:
            outb[m] = piece.astype(bf16)
            tcopy(m).start()
        else:
            total = piece
    for m in range(nt - 1):
        tcopy(m).wait_recv()
        total = total + rcv[m].astype(f32)
    out[...] = total

    for m in range(nt - 1):
        tcopy(m).wait_send()
    for q in range(2):
        lcopy(q).wait_send()
        ycopy2(q).wait_send()

    def drain(s, carry):
        for q in range(2):
            dcopy(s, q).wait_send()
            pcopy(s, q).wait_send()
            dcopy2(s, q, 0).wait_send()
            dcopy2(s, q, 1).wait_send()
            ecopy2(s, q).wait_send()
            pcopy2(s, q).wait_send()
        return carry

    def drain_ring(s, carry):
        for q in range(2):
            for n in range(3):
                rcopy(s, q, n).wait_send()
                rcopy2(s, q, n).wait_send()
        return carry

    lax.fori_loop(0, nz, drain, 0)
    lax.fori_loop(0, nz - 1, drain_ring, 0)


def table(pattern, owners, dp_devices, slots, row_blocks, col_blocks):
    keep = pattern.shape[1]
    total = row_blocks * keep
    n_dense = row_blocks * col_blocks
    n_slots = dp_devices * slots
    owner = owners.reshape(total)
    number = jnp.arange(total, dtype=jnp.int32)
    same = owner[:, None] == owner[None, :]
    earlier = number[None, :] < number[:, None]
    target = owner * slots + jnp.sum((same & earlier).astype(jnp.int32), axis=1)
    where = pattern.reshape(total) * row_blocks + number // keep
    row = jnp.arange(n_slots + n_dense + 1, dtype=jnp.int32)[:, None]
    first, last = row < n_slots, row == n_slots + n_dense
    mine = owner == lax.axis_index("dp")
    hit = jnp.where(first, target[None, :] == row, jnp.where(last, mine[None, :], where[None, :] == row - n_slots))
    value = jnp.where(first, where[None, :] - n_dense, jnp.where(last, 1, target[None, :] - n_dense))
    return jnp.where(last[:, 0], 0, n_dense) + jnp.sum(jnp.where(hit, value, 0), axis=1)


def finish_kernel(cnt, total, grads, m1, m2, out, new1, new2):
    out[...] = total[...].astype(bf16)
    for k in range(grads.shape[0]):
        new1[k], new2[k] = moments(grads[k], k < cnt[cnt.shape[0] - 1], m1[k], m2[k])


def per_device(hidden, cotangent, weight_slots, pattern, owners, first_moment, second_moment, next_hidden):
    tokens, width = hidden.shape
    cols = cotangent.shape[1]
    row_blocks = pattern.shape[0]
    slots = first_moment.shape[2]
    n_dp, n_t = lax.axis_size("dp"), lax.axis_size("tensor")
    nz, nx = n_dp // 4, n_t // 2
    col_blocks = cols * n_t // BLK
    hs = slots // 2
    next_rows = next_hidden.shape[0]
    tab = table(pattern, owners, n_dp, slots, row_blocks, col_blocks)

    vmem = pl.BlockSpec(memory_space=pltpu.VMEM)
    smem = pl.BlockSpec(memory_space=pltpu.SMEM)
    anywhere = pl.BlockSpec(memory_space=pl.ANY)
    dma = pltpu.SemaphoreType.DMA
    block = (slots, BLK, BLK)

    def pairs(*shapes):
        return [dma(shape) for shape in shapes for _ in range(2)]

    next_out, grads = pl.pallas_call(
        functools.partial(kernel, nz, nx, slots, row_blocks),
        out_shape=(
            jax.ShapeDtypeStruct((next_rows, cols), f32),
            jax.ShapeDtypeStruct(block, f32),
        ),
        in_specs=[smem, vmem] + [anywhere] * 5,
        out_specs=(vmem, vmem),
        scratch_shapes=[
            pltpu.VMEM((tokens, width), bf16),
            pltpu.VMEM(block, bf16),
            pltpu.VMEM(block, f32),
            pltpu.VMEM(block, f32),
            pltpu.VMEM((next_rows, width), bf16),
            pltpu.VMEM((n_t * tokens, cols), bf16),
            pltpu.VMEM((row_blocks * col_blocks + 1, BLK, BLK), bf16),
            pltpu.VMEM((2, width, cols), f32),
            pltpu.VMEM((nz, 2, slots, BLK, BLK), bf16),
            pltpu.VMEM((nz, 2, slots, BLK, BLK), bf16),
            pltpu.VMEM((nz - 1, 2, hs + ZF, BLK, BLK), bf16),
            pltpu.VMEM((nz, 2, hs - ZF, BLK, BLK), bf16),
            pltpu.VMEM((2, ZF, BLK, BLK), bf16),
            pltpu.VMEM((n_t - 1, next_rows, cols), bf16),
            pltpu.VMEM((n_t - 1, next_rows, cols), bf16),
            dma((5,)),
            pltpu.SemaphoreType.REGULAR,
        ]
        + pairs((CHUNKS,), (2, 2, CHUNKS), (2, CHUNKS), (2, CHUNKS))
        + pairs((nz, 2), (nz - 1, 2, 3), (nz, 2), (2,))
        + pairs((2,), (nz, 2), (nz - 1, 2, 3), (nz, 2, 2), (nz, 2), (n_t - 1,)),
        compiler_params=pltpu.CompilerParams(
            collective_id=0, has_side_effects=True, vmem_limit_bytes=60 * 1024 * 1024
        ),
        name="step",
    )(
        tab, cotangent,
        hidden, weight_slots[0, 0], first_moment[0, 0], second_moment[0, 0], next_hidden,
    )
    next_out, new1, new2 = pl.pallas_call(
        finish_kernel,
        out_shape=(
            jax.ShapeDtypeStruct((next_rows, cols), bf16),
            jax.ShapeDtypeStruct(block, f32),
            jax.ShapeDtypeStruct(block, f32),
        ),
        in_specs=[smem] + [vmem] * 4,
        out_specs=(vmem, vmem, vmem),
        name="finish",
    )(tab, next_out, grads, first_moment[0, 0], second_moment[0, 0])
    return next_out, new1[None, None], new2[None, None]


def solution(mesh):
    in_specs = (
        P("dp", "tensor"),
        P("dp", "tensor"),
        P("tensor", "dp", None, None, None),
        P("tensor", None),
        P("tensor", None, None),
        P("tensor", "dp", None, None, None),
        P("tensor", "dp", None, None, None),
        P("dp", "tensor"),
    )
    out_specs = (
        P("dp", "tensor"),
        P("tensor", "dp", None, None, None),
        P("tensor", "dp", None, None, None),
    )
    return jax.shard_map(
        per_device, mesh=mesh, in_specs=in_specs, out_specs=out_specs, check_vma=False
    )
```

```python
import functools

import jax
import jax.numpy as jnp
from jax import lax
from jax.experimental import pallas as pl
from jax.experimental.pallas import tpu as pltpu
from jax.sharding import PartitionSpec as P

ADAM_STEP = 20
BETA_ONE = 0.9
BETA_TWO = 0.95
LEARN_RATE = 0.003
EPSILON = 1e-08

BLK = 128
CHUNKS = 4

ZF = 2
MESH = pl.DeviceIdType.MESH
f32 = jnp.float32
bf16 = jnp.bfloat16


def remote(src, dst, send, recv, where):
    return pltpu.make_async_remote_copy(
        src_ref=src, dst_ref=dst, send_sem=send, recv_sem=recv, device_id=where, device_id_type=MESH
    )


def greet(places, loads):
    barrier = pltpu.get_barrier_semaphore()
    for where in places:
        pl.semaphore_signal(barrier, inc=1, device_id=where, device_id_type=MESH)
    for load in loads:
        load.start()
    pl.semaphore_wait(barrier, len(places))


class Place:
    def __init__(self, nz, nx):
        self.nz, self.nx = nz, nx
        self.d = lax.axis_index("dp")
        self.t = lax.axis_index("tensor")
        self.z = lax.div(self.d, 4)
        self.yl = lax.rem(lax.div(self.d, 2), 2)
        self.core = lax.rem(self.d, 2)
        self.x = lax.div(self.t, 2)
        self.yh = lax.rem(self.t, 2)

    def dp_of(self, z, yl, core):
        return (z * 2 + yl) * 2 + core

    def tensor_of(self, x, yh):
        return x * 2 + yh

    def x_step(self, k):
        return lax.rem(self.x + (k + self.nx), self.nx)

    def z_step(self, k):
        return lax.rem(self.z + (k + self.nz), self.nz)


def moments(grad, used, one, two):
    one = jnp.where(used, BETA_ONE * one + (1 - BETA_ONE) * grad, 0.0)
    two = jnp.where(used, BETA_TWO * two + (1 - BETA_TWO) * grad * grad, 0.0)
    return one, two


def kernel(
    nz, nx, slots, row_blocks,
    tab_in, cot, hid_in, wgt_in, m1_in, m2_in, nxt_in,
    out, grads,
    tab, hid, wgt, m1, m2, nxt,
    cotbuf, dense, acc, sendb, recvb, ringb, ybuf, yrecv, outb, rcv,
    ins, free,
    ys, yr, xs, xr, fs, fr, os, orr, gs, gr,
    ds, dr, rs, rr, ps, pr, ls, lr,
    ys2, yr2, ps2, pr2, rs2, rr2, ds2, dr2, es, er, ts, tr,
):
    me = Place(nz, nx)
    nt = 2 * nx
    tokens = cot.shape[0]
    width = hid.shape[1]
    rows = tokens // CHUNKS
    half = rows // 2
    early, late = tokens // 2, tokens - rows
    last = CHUNKS - 1
    n_dense = dense.shape[0] - 1
    n_slots = nz * 4 * slots
    hs = slots // 2

    own = cotbuf.at[pl.ds(me.t * tokens, tokens)]
    moves = [(cot, own), (hid_in, hid), (tab_in, tab), (wgt_in, wgt), (m1_in, m1), (m2_in, m2), (nxt_in, nxt)]
    loads = [pltpu.make_async_copy(src, dst, ins.at[i]) for i, (src, dst) in enumerate(moves)]
    y_far = {"tensor": me.tensor_of(me.x, 1 - me.yh)}
    x_next = [{"tensor": me.tensor_of(me.x_step(1), me.yh)}, {"tensor": me.tensor_of(me.x_step(-1), me.yh)}]
    z_next = [{"dp": me.dp_of(me.z_step(1), me.yl, me.core)}, {"dp": me.dp_of(me.z_step(-1), me.yl, me.core)}]
    y_near = {"dp": me.dp_of(me.z, 1 - me.yl, me.core)}
    twin = {"dp": me.dp_of(me.z, me.yl, 1 - me.core)}
    near = z_next + [y_near, twin]
    away = [(2, 1), (1, 1), (nx - 1, 1), (0, 1), (2, 0), (1, 0), (nx - 1, 0)]
    t_away = [me.tensor_of(me.x_step(dx), 1 - me.yh if far else me.yh) for dx, far in away] + [me.t]
    peers = [{"tensor": t_away[m]} for m in range(nt - 1)]
    greet(near + peers, loads)

    t_item = [me.t, me.tensor_of(me.x, 1 - me.yh)]
    x_opp = me.x_step(2)
    t_opp = [me.tensor_of(x_opp, me.yh), me.tensor_of(x_opp, 1 - me.yh)]

    def t_from(item, q):
        yh = me.yh if item == 0 else 1 - me.yh
        return me.tensor_of(me.x_step(-1 if q == 0 else 1), yh)

    def held(t, lo, n):
        return cotbuf.at[pl.ds(t * tokens + lo, n)]

    def ycopy(c):
        return remote(cot.at[pl.ds(c * rows, rows)], held(me.t, c * rows, rows), ys.at[c], yr.at[c], y_far)

    def xcopy(item, q, c):
        there = held(t_item[item], c * rows, half if item == 1 and c == last else rows)
        src = cot.at[pl.ds(c * rows, rows)] if item == 0 else there
        return remote(src, there, xs.at[item, q, c], xr.at[item, q, c], x_next[q])

    def fcopy(q, c):
        there = held(t_from(0, q), c * rows + q * half, half)
        return remote(there, there, fs.at[q, c], fr.at[q, c], x_next[q])

    def ocopy(q, c):
        there = held(t_opp[0], c * rows + q * half, half)
        return remote(there, there, os.at[q, c], orr.at[q, c], y_far)

    def gcopy(q):
        there = held(t_from(0, q), last * rows + half, half)
        return remote(there, there, gs.at[q], gr.at[q], y_far)

    def group(src, tq, lo=0, hi=tokens, keep=None, plus=None):
        for i in range(row_blocks // 2):
            wide = slice(i * 256, (i + 1) * 256)
            got_here = lax.dot_general(
                hid[lo:hi, wide], src[lo:hi, :], (((0,), (0,)), ((), ())), preferred_element_type=f32
            )
            if plus is not None:
                got_here = got_here + acc[plus, wide, :]
            if keep is not None:
                acc[keep, wide, :] = got_here
                continue
            for b in range(4):
                for a in range(2):
                    dense[(tq * 4 + b) * row_blocks + 2 * i + a] = got_here[
                        a * BLK : (a + 1) * BLK, b * BLK : (b + 1) * BLK
                    ].astype(bf16)

    def group_of(t, **how):
        group(held(t, 0, tokens), t, **how)

    queue = [functools.partial(xcopy, 0, c=0), functools.partial(xcopy, 0, c=1)]
    for c in range(CHUNKS):
        queue.append(functools.partial(fcopy, c=c))
        if c + 2 < CHUNKS:
            queue.append(functools.partial(xcopy, 0, c=c + 2))
        if c == CHUNKS - 2:
            queue.append(functools.partial(xcopy, 1, c=0))
    queue += [functools.partial(xcopy, 1, c=c) for c in range(1, CHUNKS)]

    def go(k):
        for q in range(2):
            queue[k](q=q).start()

    def got(k):
        for q in range(2):
            queue[k](q=q).wait_recv()
        if k + 2 < len(queue):
            go(k + 2)

    def across(c):
        for q in range(2):
            ocopy(q, c).start()

    go(0)
    ycopy(0).start()
    go(1)
    ycopy(1).start()
    dense[n_dense] = jnp.zeros((BLK, BLK), bf16)
    for load in loads[:3]:
        load.wait()
    group(own, me.t)
    got(0)
    ycopy(0).wait_recv()
    ycopy(2).start()
    got(1)
    ycopy(1).wait_recv()
    got(2)
    across(0)
    got(3)
    ycopy(2).wait_recv()
    ycopy(3).start()
    got(4)
    across(1)
    got(5)
    for q in range(2):
        gcopy(q).start()
    group_of(t_from(0, 0))
    got(6)
    across(2)
    group_of(t_from(0, 1))
    ycopy(3).wait_recv()
    got(7)
    group_of(t_item[1])
    got(8)
    across(3)
    group_of(t_opp[0])
    got(9)
    for q in range(2):
        group_of(t_from(1, q), hi=early, keep=q)
    for q in range(2):
        for c in range(CHUNKS):
            ocopy(q, c).wait_recv()
    group_of(t_opp[1])
    got(10)
    for q in range(2):
        group_of(t_from(1, q), lo=early, hi=late, keep=q, plus=q)
    got(11)
    for q in range(2):
        gcopy(q).wait_recv()
        group_of(t_from(1, q), lo=late, plus=q)

    yf = hs - ZF
    order = [(0, i) for i in range(ZF, hs)] + [(0, i) for i in range(ZF)] + [(1, i) for i in range(hs)]
    part = [(yf, hs), (hs, hs + ZF), (hs + ZF, 2 * hs)]

    def dest_z(s, q):
        return lax.rem(me.z + (2 * nz - 1 - s), nz) if q == 0 else lax.rem(me.z + 1 + s, nz)

    def pick(s, q, p, core):
        u, i = order[p]
        yl = 1 - me.yl if u == 0 else me.yl
        return dense[tab[me.dp_of(dest_z(s, q), yl, core) * slots + q * hs + i]]

    def dcopy(s, q):
        return remote(sendb.at[s, q], recvb.at[s, q], ds.at[s, q], dr.at[s, q], twin)

    def pcopy(s, q):
        return remote(recvb.at[s, q, pl.ds(0, yf)], ybuf.at[s, q], ps.at[s, q], pr.at[s, q], y_near)

    def rcopy(s, q, n):
        lo, hi = part[n]
        return remote(
            recvb.at[s, q, pl.ds(lo, hi - lo)], ringb.at[s, q, pl.ds(lo - yf, hi - lo)],
            rs.at[s, q, n], rr.at[s, q, n], z_next[q],
        )

    def lcopy(q):
        return remote(recvb.at[nz - 1, q, pl.ds(yf, ZF)], yrecv.at[q], ls.at[q], lr.at[q], y_near)

    def fill(s):
        for q in range(2):
            for p in range(2 * hs):
                sendb[s, q, p] = pick(s, q, p, 1 - me.core)
            dcopy(s, q).start()

    def spread(s):
        for q in range(2):
            dcopy(s, q).wait_recv()
            for p in range(yf):
                recvb[s, q, p] = (recvb[s, q, p].astype(f32) + pick(s, q, p, me.core).astype(f32)).astype(bf16)
            pcopy(s, q).start()

    def add(s, q, n, first=False):
        lo, hi = part[n]
        for p in range(lo, hi):
            v = recvb[s, q, p].astype(f32) + pick(s, q, p, me.core).astype(f32)
            if n == 2:
                v = v + ybuf[s, q, p - lo].astype(f32)
            if not first:
                v = v + ringb[s - 1, q, p - yf].astype(f32)
            recvb[s, q, p] = v.astype(bf16)

    def hop_ahead(s):
        for n in range(2):
            for q in range(2):
                rcopy(s - 1, q, n).wait_recv()
                add(s, q, n)
                rcopy(s, q, n).start()

    def hop_behind(s):
        for q in range(2):
            rcopy(s - 1, q, 2).wait_recv()
            pcopy(s, q).wait_recv()
            add(s, q, 2)
            rcopy(s, q, 2).start()

    fill(0)
    fill(1)
    spread(0)
    fill(2)
    for n in range(2):
        for q in range(2):
            add(0, q, n, True)
            rcopy(0, q, n).start()
    spread(1)
    fill(3)
    hop_ahead(1)
    for q in range(2):
        pcopy(0, q).wait_recv()
        add(0, q, 2, True)
        rcopy(0, q, 2).start()

    def ring(s, carry):
        spread(s)
        fill(s + 2)
        hop_ahead(s)
        hop_behind(s - 1)
        return carry

    lax.fori_loop(2, nz - 2, ring, 0)
    spread(nz - 2)
    hop_ahead(nz - 2)
    hop_behind(nz - 3)
    spread(nz - 1)
    for n in range(2):
        for q in range(2):
            rcopy(nz - 2, q, n).wait_recv()
            add(nz - 1, q, n)
            if n == 0:
                lcopy(q).start()
    hop_behind(nz - 2)
    for q in range(2):
        rcopy(nz - 2, q, 2).wait_recv()
        pcopy(nz - 1, q).wait_recv()
        add(nz - 1, q, 2)

    for where in near:
        pl.semaphore_signal(free, inc=1, device_id=where, device_id_type=MESH)

    pan = dense
    scale_one = 1.0 - BETA_ONE**ADAM_STEP
    scale_two = 1.0 - BETA_TWO**ADAM_STEP
    mine = tab[n_slots + n_dense]
    for load in loads[3:]:
        load.wait()

    def adam(q, i):
        k = q * hs + i
        grad = recvb[nz - 1, q, hs + i].astype(f32)
        if i < ZF:
            grad = grad + yrecv[q, i].astype(f32)
        grads[k] = grad
        one, two = moments(grad, k < mine, m1[k], m2[k])
        step = LEARN_RATE * (one / scale_one) / (jnp.sqrt(two / scale_two) + EPSILON)
        pan[me.d * slots + k] = (wgt[k].astype(f32) - step).astype(bf16)

    for q in range(2):
        for i in range(ZF, hs):
            adam(q, i)
    pl.semaphore_wait(free, len(near))

    def place(s, q, u, lo, n):
        z = lax.rem(me.z + (2 * nz - s), nz) if q == 0 else lax.rem(me.z + s, nz)
        yl = me.yl if u == 0 else 1 - me.yl
        return pan.at[pl.ds(me.dp_of(z, yl, me.core) * slots + q * hs + lo, n)]

    pieces = [(0, 0, ZF), (0, ZF, hs - ZF), (1, 0, ZF)]

    def ycopy2(q):
        here = place(0, q, 0, 0, ZF)
        return remote(here, here, ys2.at[q], yr2.at[q], y_near)

    def pcopy2(s, q):
        here = place(s, q, 0, ZF, hs - ZF)
        return remote(here, here, ps2.at[s, q], pr2.at[s, q], y_near)

    def rcopy2(s, q, n):
        here = place(s, q, *pieces[n])
        return remote(here, here, rs2.at[s, q, n], rr2.at[s, q, n], z_next[q])

    def dcopy2(s, q, u):
        here = place(s, q, u, 0, hs if u == 0 else ZF)
        return remote(here, here, ds2.at[s, q, u], dr2.at[s, q, u], twin)

    def ecopy2(s, q):
        here = place(s, q, 1, ZF, hs - ZF)
        return remote(here, here, es.at[s, q], er.at[s, q], twin)

    for q in range(2):
        rcopy2(0, q, 1).start()
        pcopy2(0, q).start()
    for q in range(2):
        lcopy(q).wait_recv()
        for i in range(ZF):
            adam(q, i)
        ycopy2(q).start()
        rcopy2(0, q, 0).start()
        dcopy2(0, q, 0).start()

    def ahead2(s, last=False):
        for q in range(2):
            rcopy2(s - 1, q, 1).wait_recv()
            if not last:
                rcopy2(s, q, 1).start()
            pcopy2(s, q).start()

    def behind2(s, last=False):
        for n, u in ((0, 0), (2, 1)):
            for q in range(2):
                rcopy2(s - 1, q, n).wait_recv()
                if not last:
                    rcopy2(s, q, n).start()
                dcopy2(s, q, u).start()

    def landed2(s):
        for q in range(2):
            pcopy2(s, q).wait_recv()
            ecopy2(s, q).start()

    ahead2(1)
    for q in range(2):
        ycopy2(q).wait_recv()
        rcopy2(0, q, 2).start()
        dcopy2(0, q, 1).start()
    landed2(0)

    def ring2(s, carry):
        ahead2(s)
        behind2(s - 1)
        landed2(s - 1)
        return carry

    lax.fori_loop(2, nz - 1, ring2, 0)
    ahead2(nz - 1, True)
    behind2(nz - 2)
    landed2(nz - 2)

    for c in range(CHUNKS):
        ycopy(c).wait_send()
        for q in range(2):
            for item in range(2):
                xcopy(item, q, c).wait_send()
            fcopy(q, c).wait_send()
            ocopy(q, c).wait_send()
    for q in range(2):
        gcopy(q).wait_send()

    behind2(nz - 1, True)
    landed2(nz - 1)

    def all_here(s, carry):
        for q in range(2):
            dcopy2(s, q, 0).wait_recv()
            dcopy2(s, q, 1).wait_recv()
            ecopy2(s, q).wait_recv()
        return carry

    lax.fori_loop(0, nz, all_here, 0)

    def tcopy(m):
        return remote(outb.at[m], rcv.at[m], ts.at[m], tr.at[m], peers[m])

    total = None
    for m in range(nt):
        tq = t_away[m]
        lo = (m % 2) * width

        def build(h, carry):
            for b in range(4):
                for i in range(row_blocks // 2):
                    f = h * (row_blocks // 2) + i
                    cotbuf[pl.ds(lo + f * BLK, BLK), b * BLK : (b + 1) * BLK] = pan[tab[n_slots + (tq * 4 + b) * row_blocks + f]]
            return carry

        lax.fori_loop(0, 2, build, 0)
        piece = jnp.dot(nxt[...], cotbuf[lo : lo + width, :], preferred_element_type=f32)
        if m < nt - 1:
            outb[m] = piece.astype(bf16)
            tcopy(m).start()
        else:
            total = piece
    for m in range(nt - 1):
        tcopy(m).wait_recv()
        total = total + rcv[m].astype(f32)
    out[...] = total

    for m in range(nt - 1):
        tcopy(m).wait_send()
    for q in range(2):
        lcopy(q).wait_send()
        ycopy2(q).wait_send()

    def drain(s, carry):
        for q in range(2):
            dcopy(s, q).wait_send()
            pcopy(s, q).wait_send()
            dcopy2(s, q, 0).wait_send()
            dcopy2(s, q, 1).wait_send()
            ecopy2(s, q).wait_send()
            pcopy2(s, q).wait_send()
        return carry

    def drain_ring(s, carry):
        for q in range(2):
            for n in range(3):
                rcopy(s, q, n).wait_send()
                rcopy2(s, q, n).wait_send()
        return carry

    lax.fori_loop(0, nz, drain, 0)
    lax.fori_loop(0, nz - 1, drain_ring, 0)


def table(pattern, owners, dp_devices, slots, row_blocks, col_blocks):
    keep = pattern.shape[1]
    total = row_blocks * keep
    n_dense = row_blocks * col_blocks
    n_slots = dp_devices * slots
    owner = lax.optimization_barrier(owners.reshape(total))
    number = jnp.arange(total, dtype=jnp.int32)
    same = owner[:, None] == owner[None, :]
    earlier = number[None, :] < number[:, None]
    target = owner * slots + jnp.sum((same & earlier).astype(jnp.int32), axis=1)
    where = pattern.reshape(total) * row_blocks + number // keep
    row = jnp.arange(-(-(n_slots + n_dense + 1) // 1024) * 1024, dtype=jnp.int32)[:, None]
    first, last = row < n_slots, row == n_slots + n_dense
    mine = owner == lax.axis_index("dp")
    hit = jnp.where(first, target[None, :] == row, jnp.where(last, mine[None, :], where[None, :] == row - n_slots))
    value = jnp.where(first, where[None, :] - n_dense, jnp.where(last, 1, target[None, :] - n_dense))
    return jnp.where(last[:, 0], 0, n_dense) + jnp.sum(jnp.where(hit, value, 0), axis=1)


def finish_kernel(n_last, cnt, total, grads, m1, m2, out, new1, new2):
    out[...] = total[...].astype(bf16)
    for k in range(grads.shape[0]):
        new1[k], new2[k] = moments(grads[k], k < cnt[n_last], m1[k], m2[k])


def per_device(hidden, cotangent, weight_slots, pattern, owners, first_moment, second_moment, next_hidden):
    tokens, width = hidden.shape
    cols = cotangent.shape[1]
    row_blocks = pattern.shape[0]
    slots = first_moment.shape[2]
    n_dp, n_t = lax.axis_size("dp"), lax.axis_size("tensor")
    nz, nx = n_dp // 4, n_t // 2
    col_blocks = cols * n_t // BLK
    hs = slots // 2
    next_rows = next_hidden.shape[0]
    tab = table(pattern, owners, n_dp, slots, row_blocks, col_blocks)

    vmem = pl.BlockSpec(memory_space=pltpu.VMEM)
    smem = pl.BlockSpec(memory_space=pltpu.SMEM)
    anywhere = pl.BlockSpec(memory_space=pl.ANY)
    dma = pltpu.SemaphoreType.DMA
    block = (slots, BLK, BLK)

    def pairs(*shapes):
        return [dma(shape) for shape in shapes for _ in range(2)]

    next_out, grads = pl.pallas_call(
        functools.partial(kernel, nz, nx, slots, row_blocks),
        out_shape=(
            jax.ShapeDtypeStruct((next_rows, cols), f32),
            jax.ShapeDtypeStruct(block, f32),
        ),
        in_specs=[anywhere] * 7,
        out_specs=(vmem, vmem),
        scratch_shapes=[
            pltpu.SMEM(tab.shape, jnp.int32),
            pltpu.VMEM((tokens, width), bf16),
            pltpu.VMEM(block, bf16),
            pltpu.VMEM(block, f32),
            pltpu.VMEM(block, f32),
            pltpu.VMEM((next_rows, width), bf16),
            pltpu.VMEM((n_t * tokens, cols), bf16),
            pltpu.VMEM((row_blocks * col_blocks + 1, BLK, BLK), bf16),
            pltpu.VMEM((2, width, cols), f32),
            pltpu.VMEM((nz, 2, slots, BLK, BLK), bf16),
            pltpu.VMEM((nz, 2, slots, BLK, BLK), bf16),
            pltpu.VMEM((nz - 1, 2, hs + ZF, BLK, BLK), bf16),
            pltpu.VMEM((nz, 2, hs - ZF, BLK, BLK), bf16),
            pltpu.VMEM((2, ZF, BLK, BLK), bf16),
            pltpu.VMEM((n_t - 1, next_rows, cols), bf16),
            pltpu.VMEM((n_t - 1, next_rows, cols), bf16),
            dma((7,)),
            pltpu.SemaphoreType.REGULAR,
        ]
        + pairs((CHUNKS,), (2, 2, CHUNKS), (2, CHUNKS), (2, CHUNKS), (2,))
        + pairs((nz, 2), (nz - 1, 2, 3), (nz, 2), (2,))
        + pairs((2,), (nz, 2), (nz - 1, 2, 3), (nz, 2, 2), (nz, 2), (n_t - 1,)),
        compiler_params=pltpu.CompilerParams(
            collective_id=0, has_side_effects=True, vmem_limit_bytes=60 * 1024 * 1024
        ),
        name="step",
    )(
        tab, cotangent,
        hidden, weight_slots[0, 0], first_moment[0, 0], second_moment[0, 0], next_hidden,
    )
    next_out, new1, new2 = pl.pallas_call(
        functools.partial(finish_kernel, n_dp * slots + row_blocks * col_blocks),
        out_shape=(
            jax.ShapeDtypeStruct((next_rows, cols), bf16),
            jax.ShapeDtypeStruct(block, f32),
            jax.ShapeDtypeStruct(block, f32),
        ),
        in_specs=[smem] + [vmem] * 4,
        out_specs=(vmem, vmem, vmem),
        name="finish",
    )(tab, next_out, grads, first_moment[0, 0], second_moment[0, 0])
    return next_out, new1[None, None], new2[None, None]


def solution(mesh):
    in_specs = (
        P("dp", "tensor"),
        P("dp", "tensor"),
        P("tensor", "dp", None, None, None),
        P("tensor", None),
        P("tensor", None, None),
        P("tensor", "dp", None, None, None),
        P("tensor", "dp", None, None, None),
        P("dp", "tensor"),
    )
    out_specs = (
        P("dp", "tensor"),
        P("tensor", "dp", None, None, None),
        P("tensor", "dp", None, None, None),
    )
    return jax.shard_map(
        per_device, mesh=mesh, in_specs=in_specs, out_specs=out_specs, check_vma=False
    )
```

```python
import functools

import jax
import jax.numpy as jnp
from jax import lax
from jax.experimental import pallas as pl
from jax.experimental.pallas import tpu as pltpu
from jax.sharding import PartitionSpec as P

ADAM_STEP = 20
BETA_ONE = 0.9
BETA_TWO = 0.95
LEARN_RATE = 0.003
EPSILON = 1e-08

BLK = 128
CHUNKS = 4

ZF = 2
MESH = pl.DeviceIdType.MESH
f32 = jnp.float32
bf16 = jnp.bfloat16


def remote(src, dst, send, recv, where):
    return pltpu.make_async_remote_copy(
        src_ref=src, dst_ref=dst, send_sem=send, recv_sem=recv, device_id=where, device_id_type=MESH
    )


def greet(places, loads):
    barrier = pltpu.get_barrier_semaphore()
    for where in places:
        pl.semaphore_signal(barrier, inc=1, device_id=where, device_id_type=MESH)
    for load in loads:
        load.start()
    pl.semaphore_wait(barrier, len(places))


class Place:
    def __init__(self, nz, nx):
        self.nz, self.nx = nz, nx
        self.d = lax.axis_index("dp")
        self.t = lax.axis_index("tensor")
        self.z = lax.div(self.d, 4)
        self.yl = lax.rem(lax.div(self.d, 2), 2)
        self.core = lax.rem(self.d, 2)
        self.x = lax.div(self.t, 2)
        self.yh = lax.rem(self.t, 2)

    def dp_of(self, z, yl, core):
        return (z * 2 + yl) * 2 + core

    def tensor_of(self, x, yh):
        return x * 2 + yh

    def x_step(self, k):
        return lax.rem(self.x + (k + self.nx), self.nx)

    def z_step(self, k):
        return lax.rem(self.z + (k + self.nz), self.nz)


def moments(grad, used, one, two):
    one = jnp.where(used, BETA_ONE * one + (1 - BETA_ONE) * grad, 0.0)
    two = jnp.where(used, BETA_TWO * two + (1 - BETA_TWO) * grad * grad, 0.0)
    return one, two


def kernel(
    nz, nx, slots, row_blocks,
    tab_in, cot, hid_in, wgt_in, m1_in, m2_in, nxt_in,
    out, grads,
    tab, hid, wgt, m1, m2, nxt,
    cotbuf, dense, acc, sendb, recvb, ringb, ybuf, yrecv, outb, rcv,
    ins, free,
    ys, yr, xs, xr, fs, fr, os, orr, gs, gr,
    ds, dr, rs, rr, ps, pr, ls, lr,
    ys2, yr2, ps2, pr2, rs2, rr2, ds2, dr2, es, er, ts, tr,
):
    me = Place(nz, nx)
    nt = 2 * nx
    tokens = cot.shape[0]
    width = hid.shape[1]
    rows = tokens // CHUNKS
    half = rows // 2
    early, late = tokens // 2, tokens - rows
    last = CHUNKS - 1
    n_dense = dense.shape[0] - 1
    n_slots = nz * 4 * slots
    hs = slots // 2

    own = cotbuf.at[pl.ds(me.t * tokens, tokens)]
    moves = [(cot, own), (hid_in, hid), (tab_in, tab), (wgt_in, wgt), (m1_in, m1), (m2_in, m2), (nxt_in, nxt)]
    loads = [pltpu.make_async_copy(src, dst, ins.at[i]) for i, (src, dst) in enumerate(moves)]
    y_far = {"tensor": me.tensor_of(me.x, 1 - me.yh)}
    x_next = [{"tensor": me.tensor_of(me.x_step(1), me.yh)}, {"tensor": me.tensor_of(me.x_step(-1), me.yh)}]
    z_next = [{"dp": me.dp_of(me.z_step(1), me.yl, me.core)}, {"dp": me.dp_of(me.z_step(-1), me.yl, me.core)}]
    y_near = {"dp": me.dp_of(me.z, 1 - me.yl, me.core)}
    twin = {"dp": me.dp_of(me.z, me.yl, 1 - me.core)}
    near = z_next + [y_near, twin]
    away = [(2, 1), (2, 0), (1, 1), (nx - 1, 1), (0, 1), (1, 0), (nx - 1, 0)]
    t_away = [me.tensor_of(me.x_step(dx), 1 - me.yh if far else me.yh) for dx, far in away] + [me.t]
    peers = [{"tensor": t_away[m]} for m in range(nt - 1)]
    greet(near + peers, loads)

    t_item = [me.t, me.tensor_of(me.x, 1 - me.yh)]
    x_opp = me.x_step(2)
    t_opp = [me.tensor_of(x_opp, me.yh), me.tensor_of(x_opp, 1 - me.yh)]

    def t_from(item, q):
        yh = me.yh if item == 0 else 1 - me.yh
        return me.tensor_of(me.x_step(-1 if q == 0 else 1), yh)

    def held(t, lo, n):
        return cotbuf.at[pl.ds(t * tokens + lo, n)]

    def ycopy(c):
        return remote(cot.at[pl.ds(c * rows, rows)], held(me.t, c * rows, rows), ys.at[c], yr.at[c], y_far)

    def xcopy(item, q, c):
        there = held(t_item[item], c * rows, half if item == 1 and c == last else rows)
        src = cot.at[pl.ds(c * rows, rows)] if item == 0 else there
        return remote(src, there, xs.at[item, q, c], xr.at[item, q, c], x_next[q])

    def fcopy(q, c):
        there = held(t_from(0, q), c * rows + q * half, half)
        return remote(there, there, fs.at[q, c], fr.at[q, c], x_next[q])

    def ocopy(q, c):
        there = held(t_opp[0], c * rows + q * half, half)
        return remote(there, there, os.at[q, c], orr.at[q, c], y_far)

    def gcopy(q):
        there = held(t_from(0, q), last * rows + half, half)
        return remote(there, there, gs.at[q], gr.at[q], y_far)

    def group(src, tq, lo=0, hi=tokens, keep=None, plus=None):
        for i in range(row_blocks // 2):
            wide = slice(i * 256, (i + 1) * 256)
            got_here = lax.dot_general(
                hid[lo:hi, wide], src[lo:hi, :], (((0,), (0,)), ((), ())), preferred_element_type=f32
            )
            if plus is not None:
                got_here = got_here + acc[plus, wide, :]
            if keep is not None:
                acc[keep, wide, :] = got_here
                continue
            for b in range(4):
                for a in range(2):
                    dense[(tq * 4 + b) * row_blocks + 2 * i + a] = got_here[
                        a * BLK : (a + 1) * BLK, b * BLK : (b + 1) * BLK
                    ].astype(bf16)

    def group_of(t, **how):
        group(held(t, 0, tokens), t, **how)

    queue = [functools.partial(xcopy, 0, c=0), functools.partial(xcopy, 0, c=1)]
    for c in range(CHUNKS):
        queue.append(functools.partial(fcopy, c=c))
        if c + 2 < CHUNKS:
            queue.append(functools.partial(xcopy, 0, c=c + 2))
        if c == CHUNKS - 2:
            queue.append(functools.partial(xcopy, 1, c=0))
    queue += [functools.partial(xcopy, 1, c=c) for c in range(1, CHUNKS)]

    def go(k):
        for q in range(2):
            queue[k](q=q).start()

    def got(k):
        for q in range(2):
            queue[k](q=q).wait_recv()
        if k + 2 < len(queue):
            go(k + 2)

    def across(c):
        for q in range(2):
            ocopy(q, c).start()

    go(0)
    ycopy(0).start()
    go(1)
    ycopy(1).start()
    dense[n_dense] = jnp.zeros((BLK, BLK), bf16)
    for load in loads[:3]:
        load.wait()
    group(own, me.t)
    got(0)
    ycopy(0).wait_recv()
    ycopy(2).start()
    got(1)
    ycopy(1).wait_recv()
    got(2)
    across(0)
    got(3)
    ycopy(2).wait_recv()
    ycopy(3).start()
    got(4)
    across(1)
    got(5)
    for q in range(2):
        gcopy(q).start()
    group_of(t_from(0, 0))
    got(6)
    across(2)
    group_of(t_from(0, 1))
    ycopy(3).wait_recv()
    got(7)
    group_of(t_item[1])
    got(8)
    across(3)
    group_of(t_opp[0])
    got(9)
    for q in range(2):
        group_of(t_from(1, q), hi=early, keep=q)
    for q in range(2):
        for c in range(CHUNKS):
            ocopy(q, c).wait_recv()
    group_of(t_opp[1])
    got(10)
    for q in range(2):
        group_of(t_from(1, q), lo=early, hi=late, keep=q, plus=q)
    got(11)
    for q in range(2):
        gcopy(q).wait_recv()
        group_of(t_from(1, q), lo=late, plus=q)

    yf = hs - ZF
    order = [(0, i) for i in range(ZF, hs)] + [(0, i) for i in range(ZF)] + [(1, i) for i in range(hs)]
    part = [(yf, hs), (hs, hs + ZF), (hs + ZF, 2 * hs)]

    def dest_z(s, q):
        return lax.rem(me.z + (2 * nz - 1 - s), nz) if q == 0 else lax.rem(me.z + 1 + s, nz)

    def pick(s, q, p, core):
        u, i = order[p]
        yl = 1 - me.yl if u == 0 else me.yl
        return dense[tab[me.dp_of(dest_z(s, q), yl, core) * slots + q * hs + i]]

    def dcopy(s, q):
        return remote(sendb.at[s, q], recvb.at[s, q], ds.at[s, q], dr.at[s, q], twin)

    def pcopy(s, q):
        return remote(recvb.at[s, q, pl.ds(0, yf)], ybuf.at[s, q], ps.at[s, q], pr.at[s, q], y_near)

    def rcopy(s, q, n):
        lo, hi = part[n]
        return remote(
            recvb.at[s, q, pl.ds(lo, hi - lo)], ringb.at[s, q, pl.ds(lo - yf, hi - lo)],
            rs.at[s, q, n], rr.at[s, q, n], z_next[q],
        )

    def lcopy(q):
        return remote(recvb.at[nz - 1, q, pl.ds(yf, ZF)], yrecv.at[q], ls.at[q], lr.at[q], y_near)

    def fill(s):
        for q in range(2):
            for p in range(2 * hs):
                sendb[s, q, p] = pick(s, q, p, 1 - me.core)
            dcopy(s, q).start()

    def spread(s):
        for q in range(2):
            dcopy(s, q).wait_recv()
            for p in range(yf):
                recvb[s, q, p] = (recvb[s, q, p].astype(f32) + pick(s, q, p, me.core).astype(f32)).astype(bf16)
            pcopy(s, q).start()

    def add(s, q, n, first=False):
        lo, hi = part[n]
        for p in range(lo, hi):
            v = recvb[s, q, p].astype(f32) + pick(s, q, p, me.core).astype(f32)
            if n == 2:
                v = v + ybuf[s, q, p - lo].astype(f32)
            if not first:
                v = v + ringb[s - 1, q, p - yf].astype(f32)
            recvb[s, q, p] = v.astype(bf16)

    def hop_ahead(s):
        for n in range(2):
            for q in range(2):
                rcopy(s - 1, q, n).wait_recv()
                add(s, q, n)
                rcopy(s, q, n).start()

    def hop_behind(s):
        for q in range(2):
            rcopy(s - 1, q, 2).wait_recv()
            pcopy(s, q).wait_recv()
            add(s, q, 2)
            rcopy(s, q, 2).start()

    fill(0)
    fill(1)
    spread(0)
    fill(2)
    for n in range(2):
        for q in range(2):
            add(0, q, n, True)
            rcopy(0, q, n).start()
    spread(1)
    fill(3)
    hop_ahead(1)
    for q in range(2):
        pcopy(0, q).wait_recv()
        add(0, q, 2, True)
        rcopy(0, q, 2).start()

    def ring(s, carry):
        spread(s)
        fill(s + 2)
        hop_ahead(s)
        hop_behind(s - 1)
        return carry

    lax.fori_loop(2, nz - 2, ring, 0)
    spread(nz - 2)
    hop_ahead(nz - 2)
    hop_behind(nz - 3)
    spread(nz - 1)
    for n in range(2):
        for q in range(2):
            rcopy(nz - 2, q, n).wait_recv()
            add(nz - 1, q, n)
            if n == 0:
                lcopy(q).start()
    hop_behind(nz - 2)
    for q in range(2):
        rcopy(nz - 2, q, 2).wait_recv()
        pcopy(nz - 1, q).wait_recv()
        add(nz - 1, q, 2)

    for where in near:
        pl.semaphore_signal(free, inc=1, device_id=where, device_id_type=MESH)

    pan = dense
    scale_one = 1.0 - BETA_ONE**ADAM_STEP
    scale_two = 1.0 - BETA_TWO**ADAM_STEP
    mine = tab[n_slots + n_dense]
    for load in loads[3:]:
        load.wait()

    def adam(q, i):
        k = q * hs + i
        grad = recvb[nz - 1, q, hs + i].astype(f32)
        if i < ZF:
            grad = grad + yrecv[q, i].astype(f32)
        grads[k] = grad
        one, two = moments(grad, k < mine, m1[k], m2[k])
        step = LEARN_RATE * (one / scale_one) / (jnp.sqrt(two / scale_two) + EPSILON)
        pan[me.d * slots + k] = (wgt[k].astype(f32) - step).astype(bf16)


    def place(s, q, u, lo, n):
        z = lax.rem(me.z + (2 * nz - s), nz) if q == 0 else lax.rem(me.z + s, nz)
        yl = me.yl if u == 0 else 1 - me.yl
        return pan.at[pl.ds(me.dp_of(z, yl, me.core) * slots + q * hs + lo, n)]

    pieces = [(0, 0, ZF), (0, ZF, hs - ZF), (1, 0, ZF)]

    def ycopy2(q):
        here = place(0, q, 0, 0, ZF)
        return remote(here, here, ys2.at[q], yr2.at[q], y_near)

    def pcopy2(s, q):
        here = place(s, q, 0, ZF, hs - ZF)
        return remote(here, here, ps2.at[s, q], pr2.at[s, q], y_near)

    def rcopy2(s, q, n):
        here = place(s, q, *pieces[n])
        return remote(here, here, rs2.at[s, q, n], rr2.at[s, q, n], z_next[q])

    def dcopy2(s, q, u):
        here = place(s, q, u, 0, hs if u == 0 else ZF)
        return remote(here, here, ds2.at[s, q, u], dr2.at[s, q, u], twin)

    def ecopy2(s, q):
        here = place(s, q, 1, ZF, hs - ZF)
        return remote(here, here, es.at[s, q], er.at[s, q], twin)

    for q in range(2):
        for i in range(ZF, hs):
            adam(q, i)
        if q == 0:
            pl.semaphore_wait(free, len(near))
        rcopy2(0, q, 1).start()
        pcopy2(0, q).start()
    for q in range(2):
        lcopy(q).wait_recv()
        for i in range(ZF):
            adam(q, i)
        ycopy2(q).start()
        rcopy2(0, q, 0).start()
        dcopy2(0, q, 0).start()

    def ahead2(s, last=False):
        for q in range(2):
            rcopy2(s - 1, q, 1).wait_recv()
            if not last:
                rcopy2(s, q, 1).start()
            pcopy2(s, q).start()

    def behind2(s, last=False):
        for n, u in ((0, 0), (2, 1)):
            for q in range(2):
                rcopy2(s - 1, q, n).wait_recv()
                if not last:
                    rcopy2(s, q, n).start()
                dcopy2(s, q, u).start()

    def landed2(s):
        for q in range(2):
            pcopy2(s, q).wait_recv()
            ecopy2(s, q).start()

    ahead2(1)
    for q in range(2):
        ycopy2(q).wait_recv()
        rcopy2(0, q, 2).start()
        dcopy2(0, q, 1).start()
    landed2(0)

    def ring2(s, carry):
        ahead2(s)
        behind2(s - 1)
        landed2(s - 1)
        return carry

    lax.fori_loop(2, nz - 1, ring2, 0)
    ahead2(nz - 1, True)
    behind2(nz - 2)
    landed2(nz - 2)

    for c in range(CHUNKS):
        ycopy(c).wait_send()
        for q in range(2):
            for item in range(2):
                xcopy(item, q, c).wait_send()
            fcopy(q, c).wait_send()
            ocopy(q, c).wait_send()
    for q in range(2):
        gcopy(q).wait_send()

    behind2(nz - 1, True)
    landed2(nz - 1)

    def all_here(s, carry):
        for q in range(2):
            dcopy2(s, q, 0).wait_recv()
            dcopy2(s, q, 1).wait_recv()
            ecopy2(s, q).wait_recv()
        return carry

    lax.fori_loop(0, nz, all_here, 0)

    def tcopy(m):
        return remote(outb.at[m], rcv.at[m], ts.at[m], tr.at[m], peers[m])

    total = None
    for m in range(nt):
        tq = t_away[m]
        lo = (m % 2) * width

        def build(h, carry):
            for b in range(4):
                for i in range(row_blocks // 2):
                    f = h * (row_blocks // 2) + i
                    cotbuf[pl.ds(lo + f * BLK, BLK), b * BLK : (b + 1) * BLK] = pan[tab[n_slots + (tq * 4 + b) * row_blocks + f]]
            return carry

        lax.fori_loop(0, 2, build, 0)
        piece = jnp.dot(nxt[...], cotbuf[lo : lo + width, :], preferred_element_type=f32)
        if m < nt - 1:
            outb[m] = piece.astype(bf16)
            tcopy(m).start()
        else:
            total = piece
    for m in range(nt - 1):
        tcopy(m).wait_recv()
        total = total + rcv[m].astype(f32)
    out[...] = total

    for m in range(nt - 1):
        tcopy(m).wait_send()
    for q in range(2):
        lcopy(q).wait_send()
        ycopy2(q).wait_send()

    def drain(s, carry):
        for q in range(2):
            dcopy(s, q).wait_send()
            pcopy(s, q).wait_send()
            dcopy2(s, q, 0).wait_send()
            dcopy2(s, q, 1).wait_send()
            ecopy2(s, q).wait_send()
            pcopy2(s, q).wait_send()
        return carry

    def drain_ring(s, carry):
        for q in range(2):
            for n in range(3):
                rcopy(s, q, n).wait_send()
                rcopy2(s, q, n).wait_send()
        return carry

    lax.fori_loop(0, nz, drain, 0)
    lax.fori_loop(0, nz - 1, drain_ring, 0)


def table(pattern, owners, dp_devices, slots, row_blocks, col_blocks):
    keep = pattern.shape[1]
    total = row_blocks * keep
    n_dense = row_blocks * col_blocks
    n_slots = dp_devices * slots
    owner = lax.optimization_barrier(owners.reshape(total))
    number = jnp.arange(total, dtype=jnp.int32)
    same = owner[:, None] == owner[None, :]
    earlier = number[None, :] < number[:, None]
    target = owner * slots + jnp.sum((same & earlier).astype(jnp.int32), axis=1)
    where = pattern.reshape(total) * row_blocks + number // keep
    row = jnp.arange(-(-(n_slots + n_dense + 1) // 1024) * 1024, dtype=jnp.int32)[:, None]
    first, last = row < n_slots, row == n_slots + n_dense
    mine = owner == lax.axis_index("dp")
    hit = jnp.where(first, target[None, :] == row, jnp.where(last, mine[None, :], where[None, :] == row - n_slots))
    value = jnp.where(first, where[None, :] - n_dense, jnp.where(last, 1, target[None, :] - n_dense))
    return jnp.where(last[:, 0], 0, n_dense) + jnp.sum(jnp.where(hit, value, 0), axis=1)


def finish_kernel(n_last, cnt, total, grads, m1, m2, out, new1, new2):
    out[...] = total[...].astype(bf16)
    for k in range(grads.shape[0]):
        new1[k], new2[k] = moments(grads[k], k < cnt[n_last], m1[k], m2[k])


def per_device(hidden, cotangent, weight_slots, pattern, owners, first_moment, second_moment, next_hidden):
    tokens, width = hidden.shape
    cols = cotangent.shape[1]
    row_blocks = pattern.shape[0]
    slots = first_moment.shape[2]
    n_dp, n_t = lax.axis_size("dp"), lax.axis_size("tensor")
    nz, nx = n_dp // 4, n_t // 2
    col_blocks = cols * n_t // BLK
    hs = slots // 2
    next_rows = next_hidden.shape[0]
    tab = table(pattern, owners, n_dp, slots, row_blocks, col_blocks)

    vmem = pl.BlockSpec(memory_space=pltpu.VMEM)
    smem = pl.BlockSpec(memory_space=pltpu.SMEM)
    anywhere = pl.BlockSpec(memory_space=pl.ANY)
    dma = pltpu.SemaphoreType.DMA
    block = (slots, BLK, BLK)

    def pairs(*shapes):
        return [dma(shape) for shape in shapes for _ in range(2)]

    next_out, grads = pl.pallas_call(
        functools.partial(kernel, nz, nx, slots, row_blocks),
        out_shape=(
            jax.ShapeDtypeStruct((next_rows, cols), f32),
            jax.ShapeDtypeStruct(block, f32),
        ),
        in_specs=[anywhere] * 7,
        out_specs=(vmem, vmem),
        scratch_shapes=[
            pltpu.SMEM(tab.shape, jnp.int32),
            pltpu.VMEM((tokens, width), bf16),
            pltpu.VMEM(block, bf16),
            pltpu.VMEM(block, f32),
            pltpu.VMEM(block, f32),
            pltpu.VMEM((next_rows, width), bf16),
            pltpu.VMEM((n_t * tokens, cols), bf16),
            pltpu.VMEM((row_blocks * col_blocks + 1, BLK, BLK), bf16),
            pltpu.VMEM((2, width, cols), f32),
            pltpu.VMEM((nz, 2, slots, BLK, BLK), bf16),
            pltpu.VMEM((nz, 2, slots, BLK, BLK), bf16),
            pltpu.VMEM((nz - 1, 2, hs + ZF, BLK, BLK), bf16),
            pltpu.VMEM((nz, 2, hs - ZF, BLK, BLK), bf16),
            pltpu.VMEM((2, ZF, BLK, BLK), bf16),
            pltpu.VMEM((n_t - 1, next_rows, cols), bf16),
            pltpu.VMEM((n_t - 1, next_rows, cols), bf16),
            dma((7,)),
            pltpu.SemaphoreType.REGULAR,
        ]
        + pairs((CHUNKS,), (2, 2, CHUNKS), (2, CHUNKS), (2, CHUNKS), (2,))
        + pairs((nz, 2), (nz - 1, 2, 3), (nz, 2), (2,))
        + pairs((2,), (nz, 2), (nz - 1, 2, 3), (nz, 2, 2), (nz, 2), (n_t - 1,)),
        compiler_params=pltpu.CompilerParams(
            collective_id=0, has_side_effects=True, vmem_limit_bytes=60 * 1024 * 1024
        ),
        name="step",
    )(
        tab, cotangent,
        hidden, weight_slots[0, 0], first_moment[0, 0], second_moment[0, 0], next_hidden,
    )
    next_out, new1, new2 = pl.pallas_call(
        functools.partial(finish_kernel, n_dp * slots + row_blocks * col_blocks),
        out_shape=(
            jax.ShapeDtypeStruct((next_rows, cols), bf16),
            jax.ShapeDtypeStruct(block, f32),
            jax.ShapeDtypeStruct(block, f32),
        ),
        in_specs=[smem] + [vmem] * 4,
        out_specs=(vmem, vmem, vmem),
        name="finish",
    )(tab, next_out, grads, first_moment[0, 0], second_moment[0, 0])
    return next_out, new1[None, None], new2[None, None]


def solution(mesh):
    in_specs = (
        P("dp", "tensor"),
        P("dp", "tensor"),
        P("tensor", "dp", None, None, None),
        P("tensor", None),
        P("tensor", None, None),
        P("tensor", "dp", None, None, None),
        P("tensor", "dp", None, None, None),
        P("dp", "tensor"),
    )
    out_specs = (
        P("dp", "tensor"),
        P("tensor", "dp", None, None, None),
        P("tensor", "dp", None, None, None),
    )
    return jax.shard_map(
        per_device, mesh=mesh, in_specs=in_specs, out_specs=out_specs, check_vma=False
    )
```
